32 devices in a mesh: seg: 16 (over z, y, x), bond: 2 (over core).
Axes of the slice: x: 2, y: 2, z: 4, core: 2. Of those that a mesh axis runs over, the one named last changes fastest.
Arguments:
- left_env: bfloat16 [16, 512, 14, 512], P('seg', 'bond'), may hold values from -0.25 to 0.25
- right_env: bfloat16 [16, 512, 14, 512], P('seg', 'bond'), may hold values from -0.25 to 0.25
- states: bfloat16 [16, 4, 512, 2, 512], P('seg', None, 'bond'), may hold values from -6 to 6
- mpo: bfloat16 [14, 2, 2, 14], replicated, may hold values from -0.3125 to 0.3125
Outputs:
- applied: bfloat16 [16, 4, 512, 2, 512], P('seg', None, 'bond')
- new_env: bfloat16 [16, 512, 14, 512], P('seg', 'bond')
The draws below stay inside these ranges and needn't reach their ends.
All inputs are finite; a program needn't handle non-finite values.
Results may differ from the reference program's by a relative error of at most 0.013.
Values may be sent and summed in bfloat16 or wider, within the bound.
No kernel may reach another device: no remote copies, remote signals or barrier semaphores. Data moves between devices by JAX's collectives and lax.ppermute only.
A program may use at most 192 MiB of HBM per device.

```python
import math
import jax
import jax.numpy as jnp
from jax import lax

CHI = 512
MW = 14
PHYS = 2
STATES = 4
SEGS = 16


def raised(array, stream_key, source, target, parts, factor):
    owner, partner = [(jnp.arange(array.shape[position]) // (array.shape[position] // parts)).reshape([-1 if axis == position else 1 for axis in range(array.ndim)]) for position in (source, target)]
    chosen = jax.random.permutation(stream_key, parts)[partner]
    strong = (owner == chosen) | (owner == (partner + parts // 2) % parts)
    return jnp.where(strong, factor * array, array)


def levels(key, dims, cuts, least, top_value):
    def one(dim, shards_of):
        steps = jax.random.uniform(jax.random.fold_in(jax.random.fold_in(key, 6), dim), (shards_of,), jnp.float32, least / len(cuts), top_value / len(cuts))
        return jnp.repeat(jnp.exp(steps), dims[dim] // shards_of).reshape((-1,) + (1,) * (len(dims) - dim - 1))

    level = one(*cuts[0])
    for cut in cuts[1:]:
        level = level * one(*cut)
    return level


def gaussian(key, extent, spread, reach, split=(), dtype=jnp.bfloat16):
    drawn = spread * jax.random.normal(key, extent, jnp.float32)
    if split:
        drawn = drawn * levels(key, extent, split, -0.22, 0.18)
    return jnp.clip(drawn, -reach, reach).astype(dtype)


def gaussian_with(key, extent, spread, limit, cuts, heavy, dtype=jnp.bfloat16):
    entries = spread * jax.random.normal(key, extent, jnp.float32)
    if cuts:
        entries = entries * levels(key, extent, cuts, -0.22, 0.18)
    return jnp.clip(raised(entries, jax.random.fold_in(key, 3), *heavy), -limit, limit).astype(dtype)


def setup_inputs(seed: int = 0) -> dict:
    splits = jax.random.split(jax.random.key(seed), 5)
    left_env = gaussian(splits[0], (SEGS, CHI, MW, CHI), CHI ** -0.5, 0.25, ((0, 16), (1, 2)))
    right_env = gaussian(splits[1], (SEGS, CHI, MW, CHI), CHI ** -0.5, 0.25, ((0, 16), (1, 2)))
    states = gaussian_with(splits[2], (SEGS, STATES, CHI, PHYS, CHI), 1.0, 6.0, ((0, 16), (2, 2)), (2, 4, 2, 2.0))
    mpo = gaussian(splits[3], (MW, PHYS, PHYS, MW), (2 * MW * MW) ** -0.5, 0.3125)
    return dict(left_env=left_env, right_env=right_env, states=states, mpo=mpo)


def one_boundary(operands):
    left_part, right_part, wave, mpo_full = operands
    highest = lax.Precision.HIGHEST
    wave_wide = wave.astype(jnp.float32)
    inner = jnp.einsum('awc,kcte->awkte', left_part.astype(jnp.float32), wave_wide, precision=highest)
    inner_low = inner.astype(jnp.bfloat16)
    inner_back = inner_low.astype(jnp.float32)
    through = jnp.einsum('wstv,awkte->aksve', mpo_full.astype(jnp.float32), inner_back, precision=highest)
    through_low = through.astype(jnp.bfloat16)
    through_back = through_low.astype(jnp.float32)
    applied = jnp.einsum('aksvc,bvc->kasb', through_back, right_part.astype(jnp.float32), precision=highest)
    scaling = 1.0 / math.sqrt(STATES * CHI)
    summed = jnp.einsum('kasb,aksve->bve', wave_wide, through_back, precision=highest) * scaling
    return (applied.astype(jnp.bfloat16), summed.astype(jnp.bfloat16))

def reference(left_env, right_env, states, mpo):
    neighbour = jnp.concatenate([right_env[1:], jnp.zeros_like(right_env[:1])], axis=0)
    mpo_copies = jnp.broadcast_to(mpo, (left_env.shape[0],) + mpo.shape)
    applied, new_env = lax.map(one_boundary, (left_env, neighbour, states, mpo_copies))
    return (applied, new_env)
```

```python
import functools
import math

import jax
import jax.numpy as jnp
from jax import lax
from jax.experimental import pallas as pl
from jax.experimental.pallas import tpu as pltpu
from jax.sharding import PartitionSpec as P

GROUP = 8
MIB = 1 << 20


def passed_along(array, axis, by):
    size = lax.axis_size(axis)
    pairs = [(i, i + by) for i in range(size) if 0 <= i + by < size]
    return lax.ppermute(array, axis, pairs)


def swapped(array, axis):
    return lax.ppermute(array, axis, [(0, 1), (1, 0)])


def product(left, right, contract):
    return lax.dot_general(left, right, (contract, ((), ())), preferred_element_type=jnp.float32)


def block_diagonal(mpo):
    mw, phys = mpo.shape[0], mpo.shape[1]
    eye = jnp.eye(GROUP, dtype=mpo.dtype)
    table = mpo.transpose(3, 1, 2, 0)[:, None, :, :, :, None] * eye[None, :, None, None, None, :]
    return table.reshape(mw * GROUP * phys, phys * mw * GROUP)


def through_kernel(parts, places, table_ref, *refs):
    envs, waves, out_ref = refs[:parts], refs[parts : 2 * parts], refs[2 * parts]
    mw, rows, _ = envs[0].shape
    num_states, phys, _, chi = waves[0].shape
    table = table_ref[...]
    for k in range(num_states):
        inner = []
        for t in range(phys):
            total = None
            for env, wave in zip(envs, waves):
                lhs = env[...].reshape(mw * rows, env.shape[2])
                term = product(lhs, wave[k, t], ((1,), (0,)))
                total = term if total is None else total + term
            inner.append(total.reshape(mw, rows // GROUP, GROUP, chi))
        for g in range(rows // GROUP):
            low = jnp.concatenate(
                [part[:, g].reshape(mw * GROUP, chi) for part in inner], axis=0
            ).astype(jnp.bfloat16)
            through = product(table, low, ((1,), (0,)))
            out_ref[:, k, g * phys * GROUP : (g + 1) * phys * GROUP, :] = through.astype(
                jnp.bfloat16
            ).reshape(mw, GROUP * phys, chi)


def through_low(table, env, waves, places):
    mw, rows_all, chi_in = env.shape
    num_states, phys, _, chi = waves[0].shape
    rows = min(32, rows_all)
    parts = len(waves)
    steps = rows_all // rows
    width = chi_in // parts

    def env_spec(part):
        return pl.BlockSpec((mw, rows, width), lambda i, at: (0, i, at[part]))

    return pl.pallas_call(
        functools.partial(through_kernel, parts),
        grid_spec=pltpu.PrefetchScalarGridSpec(
            num_scalar_prefetch=1,
            grid=(steps,),
            in_specs=[pl.BlockSpec(table.shape, lambda i, at: (0, 0))]
            + [env_spec(part) for part in range(parts)]
            + [pl.BlockSpec(wave.shape, lambda i, at: (0, 0, 0, 0)) for wave in waves],
            out_specs=pl.BlockSpec(
                (mw, num_states, rows * phys, chi), lambda i, at: (0, 0, i, 0)
            ),
        ),
        out_shape=jax.ShapeDtypeStruct((mw, num_states, rows_all * phys, chi), jnp.bfloat16),
        compiler_params=pltpu.CompilerParams(vmem_limit_bytes=48 * MIB),
        cost_estimate=pl.CostEstimate(
            flops=2 * mw * rows_all * chi_in * num_states * phys * chi * 3 // 2,
            bytes_accessed=2 * mw * num_states * rows_all * phys * chi,
            transcendentals=0,
        ),
        name="through",
    )(places, table, *([env] * parts), *waves)


def env_kernel(scaling, places, wave_ref, through_ref, *refs):
    out_ref = refs[-1]
    through = through_ref[0].reshape(wave_ref.shape[1], through_ref.shape[3])
    total = product(wave_ref[...], through, ((1,), (0,))) * scaling
    if len(refs) > 1:
        total = total + refs[0][0].astype(jnp.float32)
    out_ref[0] = total.astype(jnp.bfloat16)


def env_rows(scaling, wave_turned, through, places, which, count, arrived=None):
    mw, num_states, rows, chi = through.shape
    depth = wave_turned.shape[1]
    width = wave_turned.shape[0] // count
    arrivals = [] if arrived is None else [arrived]
    return pl.pallas_call(
        functools.partial(env_kernel, scaling),
        grid_spec=pltpu.PrefetchScalarGridSpec(
            num_scalar_prefetch=1,
            grid=(mw,),
            in_specs=[
                pl.BlockSpec((width, depth), lambda v, at: (at[which], 0)),
                pl.BlockSpec((1, num_states, rows, chi), lambda v, at: (v, 0, 0, 0)),
            ]
            + [pl.BlockSpec((1, width, chi), lambda v, at: (v, 0, 0)) for _ in arrivals],
            out_specs=pl.BlockSpec((1, width, chi), lambda v, at: (v, 0, 0)),
        ),
        out_shape=jax.ShapeDtypeStruct((mw, width, chi), jnp.bfloat16),
        compiler_params=pltpu.CompilerParams(vmem_limit_bytes=32 * MIB),
        cost_estimate=pl.CostEstimate(
            flops=2 * mw * width * depth * chi,
            bytes_accessed=2 * mw * depth * chi,
            transcendentals=0,
        ),
        name="env_rows",
    )(places, wave_turned, through, *arrivals)


def applied_kernel(parts, first, last, places, through_ref, *refs):
    rights = refs[:parts]
    sums = refs[parts : 2 * parts] if not first else [None] * parts
    outs = refs[parts if first else 2 * parts :]
    count = through_ref.shape[0]
    for part, (right, held) in enumerate(zip(rights, sums)):
        total = None if held is None else held[0]
        for v in range(count):
            term = product(through_ref[v, 0], right[v], ((1,), (1,)))
            total = term if total is None else total + term
        if last:
            width = right.shape[1]
            columns = pl.ds(pl.multiple_of(places[part] * width, width), width)
            outs[0][0, :, columns] = total.astype(jnp.bfloat16)
        else:
            outs[part][0] = total


def applied_part(through, rights, sums, at, places, last):
    mw, num_states, rows, chi = through.shape
    count = rights[0].shape[0]
    parts = len(rights)
    first = sums is None
    width = rights[0].shape[1]
    if last:
        out_shape = jax.ShapeDtypeStruct((num_states, rows, width * parts), jnp.bfloat16)
        out_specs = pl.BlockSpec((1, rows, width * parts), lambda k, at: (k, 0, 0))
    else:
        out_shape = [jax.ShapeDtypeStruct((num_states, rows, width), jnp.float32)] * parts
        out_specs = [pl.BlockSpec((1, rows, width), lambda k, at: (k, 0, 0))] * parts
    slab = at // count
    assert at % count == 0
    return pl.pallas_call(
        functools.partial(applied_kernel, parts, first, last),
        grid_spec=pltpu.PrefetchScalarGridSpec(
            num_scalar_prefetch=1,
            grid=(num_states,),
            in_specs=[pl.BlockSpec((count, 1, rows, chi), lambda k, at: (slab, k, 0, 0))]
            + [pl.BlockSpec(right.shape, lambda k, at: (0, 0, 0)) for right in rights]
            + ([] if first else [pl.BlockSpec((1, rows, width), lambda k, at: (k, 0, 0))] * parts),
            out_specs=out_specs,
        ),
        out_shape=out_shape,
        compiler_params=pltpu.CompilerParams(vmem_limit_bytes=48 * MIB),
        cost_estimate=pl.CostEstimate(
            flops=2 * num_states * rows * width * parts * count * chi,
            bytes_accessed=2 * count * num_states * rows * chi,
            transcendentals=0,
        ),
        name="applied_part",
    )(places, through, *rights, *([] if first else sums))


def cuts(size):
    if size % 7 == 0 and size > 7:
        step = size // 7
        return [(0, 2 * step), (2 * step, 2 * step), (4 * step, 2 * step), (6 * step, step)]
    return [(0, size)]


def on_device(left_env, right_env, states, mpo):
    num_states, rows, phys, chi = states.shape[1:]
    bonds = lax.axis_size("bond")
    paired = bonds == 2
    me = lax.axis_index("bond").astype(jnp.int32)
    places = jnp.stack([me, 1 - me]) if paired else jnp.stack([me, me]) * 0
    scaling = 1.0 / math.sqrt(num_states * chi)
    left = left_env[0].transpose(1, 0, 2)
    right = right_env[0].transpose(1, 0, 2)

    pieces = [
        (at, passed_along(right[at : at + count], "seg", -1)) for at, count in cuts(right.shape[0])
    ]

    wave_split = states[0].transpose(0, 2, 1, 3)
    if paired:
        waves = [wave_split, swapped(wave_split, "bond")]
    else:
        waves = [lax.all_gather(wave_split, "bond", axis=2, tiled=True)]
    wave_turned = states[0].transpose(3, 0, 1, 2).reshape(chi, num_states * rows * phys)
    through = through_low(block_diagonal(mpo), left, waves, places)

    if paired:
        sent = env_rows(scaling, wave_turned, through, places, 1, 2)
        arrived = swapped(sent, "bond")
        new_env = env_rows(scaling, wave_turned, through, places, 0, 2, arrived)
    else:
        share = env_rows(scaling, wave_turned, through, places, 0, 1)
        new_env = lax.psum_scatter(share, "bond", scatter_dimension=1, tiled=True)

    sums = None
    for index, (at, piece) in enumerate(pieces):
        if paired:
            rights = [piece, swapped(piece, "bond")]
        else:
            rights = [lax.all_gather(piece, "bond", axis=1, tiled=True)]
        sums = applied_part(through, rights, sums, at, places, index == len(pieces) - 1)
    applied = sums.reshape(num_states, rows, phys, chi)
    return (applied[None], new_env.transpose(1, 0, 2)[None])


def solution(mesh):
    in_specs = (
        P("seg", "bond", None, None),
        P("seg", "bond", None, None),
        P("seg", None, "bond", None, None),
        P(),
    )
    out_specs = (P("seg", None, "bond", None, None), P("seg", "bond", None, None))
    return jax.shard_map(
        on_device, mesh=mesh, in_specs=in_specs, out_specs=out_specs, check_vma=False
    )
```

```python
import functools
import math

import jax
import jax.numpy as jnp
from jax import lax
from jax.experimental import pallas as pl
from jax.experimental.pallas import tpu as pltpu
from jax.sharding import PartitionSpec as P

GROUP = 8
MIB = 1 << 20
ANY = pl.BlockSpec(memory_space=pl.ANY)


def passed_along(array, axis, by):
    size = lax.axis_size(axis)
    pairs = [(i, i + by) for i in range(size) if 0 <= i + by < size]
    return lax.ppermute(array, axis, pairs)


def swapped(array, axis):
    return lax.ppermute(array, axis, [(0, 1), (1, 0)])


def product(left, right, contract):
    return lax.dot_general(left, right, (contract, ((), ())), preferred_element_type=jnp.float32)


def after(array, *others):
    return pl.pallas_call(
        lambda *refs: None,
        in_specs=[ANY] * (1 + len(others)),
        out_specs=ANY,
        out_shape=jax.ShapeDtypeStruct(array.shape, array.dtype),
        input_output_aliases={0: 0},
        name="after",
    )(array, *others)


def block_diagonal(bonds, mw, phys):
    size = mw * phys
    full = size * GROUP
    row = lax.broadcasted_iota(jnp.int32, (full, size), 0)
    which = lax.broadcasted_iota(jnp.int32, (full, size), 1)
    pick_row = (row // (GROUP * phys) * phys + row % phys == which).astype(jnp.bfloat16)
    column = lax.broadcasted_iota(jnp.int32, (size, full), 1)
    which = lax.broadcasted_iota(jnp.int32, (size, full), 0)
    pick_column = (column // GROUP == which).astype(jnp.bfloat16)
    spread = product(pick_row, bonds, ((1,), (0,))).astype(jnp.bfloat16)
    spread = product(spread, pick_column, ((1,), (0,)))
    row = lax.broadcasted_iota(jnp.int32, (full, full), 0)
    column = lax.broadcasted_iota(jnp.int32, (full, full), 1)
    same = row % (GROUP * phys) // phys == column % GROUP
    return jnp.where(same, spread, 0.0).astype(jnp.bfloat16)


def sweep_kernel(parts, scaling, places, bonds_ref, *refs):
    envs, refs = refs[:parts], refs[parts:]
    waves, refs = refs[:parts], refs[parts:]
    here_ref, through_ref, refs = refs[0], refs[1], refs[2:]
    outs, refs = refs[:parts], refs[parts:]
    table, lhs, low, turned, total, stage, sems = refs
    mw, rows, _ = envs[0].shape
    num_states, phys, _, chi = waves[0].shape
    groups = rows // GROUP
    part = mw * GROUP
    step, steps = pl.program_id(0), pl.num_programs(0)

    @pl.when(step == 0)
    def _():
        table[...] = block_diagonal(bonds_ref[...], mw, phys)

    env = jnp.concatenate([env[...] for env in envs], axis=2).astype(jnp.float32)
    env = env.reshape(mw, groups, GROUP, chi)
    for g in range(groups):
        lhs[g * part : (g + 1) * part, :] = env[:, g].reshape(part, chi).astype(jnp.bfloat16)
    depth = rows * phys
    for k in range(num_states):
        turned[:, k * depth : (k + 1) * depth] = here_ref[k].T

    def state(k, _):
        for t in range(phys):
            wave = jnp.concatenate([wave[k, t] for wave in waves], axis=0)
            low[t] = product(lhs[...], wave, ((1,), (0,))).astype(jnp.bfloat16)
        for g in range(groups):
            right = jnp.concatenate([low[t, g * part : (g + 1) * part] for t in range(phys)], axis=0)
            through = product(table[...], right, ((1,), (0,))).astype(jnp.bfloat16)
            size = GROUP * phys
            through_ref[:, k, g * size : (g + 1) * size, :] = through.reshape(mw, size, chi)
        return 0

    lax.fori_loop(0, num_states, state, 0)

    def copies(v, slot):
        found = []
        for index, out in enumerate(outs):
            width = out.shape[1]
            at = pl.multiple_of(places[index] * width, width)
            found.append(
                pltpu.make_async_copy(
                    stage.at[slot, pl.ds(at, width)], out.at[v], sems.at[slot, index]
                )
            )
        return found

    def bond(v, _):
        right = through_ref[v].reshape(num_states * depth, chi)
        before = jnp.where(step == 0, 0.0, total[v])
        now = before + product(turned[...], right, ((1,), (0,)))

        @pl.when(step < steps - 1)
        def _():
            total[v] = now

        @pl.when(step == steps - 1)
        def _():
            slot = v % 2

            @pl.when(v >= 2)
            def _():
                for copy in copies(v - 2, slot):
                    copy.wait()

            stage[slot] = (now * scaling).astype(jnp.bfloat16)
            for copy in copies(v, slot):
                copy.start()

        return 0

    lax.fori_loop(0, mw, bond, 0)

    @pl.when(step == steps - 1)
    def _():
        for v in range(max(mw - 2, 0), mw):
            for copy in copies(v, v % 2):
                copy.wait()


def sweep(bonds, env, waves, here, places, scaling):
    mw, rows_all, chi_in = env.shape
    num_states, phys, _, chi = waves[0].shape
    rows = min(64, rows_all)
    parts = len(waves)
    width = chi_in // parts
    once = pl.Buffered(1)

    def env_spec(part):
        return pl.BlockSpec((mw, rows, width), lambda i, at: (0, i, at[part]))

    share = jax.ShapeDtypeStruct((mw, chi // parts, chi), jnp.bfloat16)
    return pl.pallas_call(
        functools.partial(sweep_kernel, parts, scaling),
        grid_spec=pltpu.PrefetchScalarGridSpec(
            num_scalar_prefetch=1,
            grid=(rows_all // rows,),
            in_specs=[pl.BlockSpec(bonds.shape, lambda i, at: (0, 0), pipeline_mode=once)]
            + [env_spec(part) for part in range(parts)]
            + [
                pl.BlockSpec(wave.shape, lambda i, at: (0, 0, 0, 0), pipeline_mode=once)
                for wave in waves
            ]
            + [pl.BlockSpec((num_states, rows * phys, chi), lambda i, at: (0, i, 0))],
            out_specs=[
                pl.BlockSpec((mw, num_states, rows * phys, chi), lambda i, at: (0, 0, i, 0))
            ]
            + [ANY] * parts,
            scratch_shapes=[
                pltpu.VMEM((mw * phys * GROUP, mw * phys * GROUP), jnp.bfloat16),
                pltpu.VMEM((mw * rows, chi_in), jnp.bfloat16),
                pltpu.VMEM((phys, mw * rows, chi), jnp.bfloat16),
                pltpu.VMEM((chi, num_states * rows * phys), jnp.bfloat16),
                pltpu.VMEM((mw, chi, chi), jnp.float32),
                pltpu.VMEM((2, chi, chi), jnp.bfloat16),
                pltpu.SemaphoreType.DMA((2, parts)),
            ],
        ),
        out_shape=[
            jax.ShapeDtypeStruct((mw, num_states, rows_all * phys, chi), jnp.bfloat16)
        ]
        + [share] * parts,
        compiler_params=pltpu.CompilerParams(vmem_limit_bytes=56 * MIB),
        cost_estimate=pl.CostEstimate(
            flops=5 * mw * rows_all * chi_in * num_states * phys * chi,
            bytes_accessed=2 * mw * num_states * rows_all * phys * chi,
            transcendentals=0,
        ),
        name="sweep",
    )(places, bonds, *([env] * parts), *waves, here)


def applied_kernel(begun, phys, places, through_ref, right_ref, *refs):
    out_ref = refs[-1]
    last = out_ref.dtype == jnp.bfloat16
    v = pl.program_id(1)
    for k in range(through_ref.shape[1]):
        term = product(through_ref[0, k], right_ref[0], ((1,), (1,)))
        if last:
            term = term + refs[0][k] if begun else term
            rows, width = term.shape
            out_ref[k] = term.astype(jnp.bfloat16).reshape(rows // phys, phys, width)
        elif begun:
            out_ref[k] = term + jnp.where(v == 0, refs[0][k], out_ref[k])
        else:
            out_ref[k] = term + jnp.where(v == 0, 0.0, out_ref[k])


def applied_part(through, right, held, at, places, part, phys, last, earlier):
    mw, num_states, rows, chi = through.shape
    count, width, _ = right.shape
    together = 1 if count == 1 else num_states
    begun = held is not None
    if last:
        assert count == 1
        out_shape = jax.ShapeDtypeStruct((num_states, rows // phys, phys, chi), jnp.bfloat16)
        out_spec = pl.BlockSpec(
            (together, rows // phys, phys, width), lambda j, v, at: (j, 0, 0, at[part])
        )
    else:
        out_shape = jax.ShapeDtypeStruct((num_states, rows, width), jnp.float32)
        out_spec = pl.BlockSpec((together, rows, width), lambda j, v, at: (j, 0, 0))
    operands = [through, right]
    in_specs = [
        pl.BlockSpec((1, together, rows, chi), lambda j, v, _: (at + v, j, 0, 0)),
        pl.BlockSpec((1, width, chi), lambda j, v, _: (v, 0, 0)),
    ]
    if begun:
        operands.append(held)
        in_specs.append(pl.BlockSpec((together, rows, width), lambda j, v, _: (j, 0, 0)))
    aliases = {}
    if earlier is not None:
        if last and earlier.shape == out_shape.shape:
            aliases = {1 + len(operands): 0}
        operands.append(earlier)
        in_specs.append(ANY)
    return pl.pallas_call(
        functools.partial(applied_kernel, begun, phys),
        grid_spec=pltpu.PrefetchScalarGridSpec(
            num_scalar_prefetch=1,
            grid=(num_states // together, count),
            in_specs=in_specs,
            out_specs=out_spec,
        ),
        out_shape=out_shape,
        input_output_aliases=aliases,
        compiler_params=pltpu.CompilerParams(vmem_limit_bytes=32 * MIB),
        cost_estimate=pl.CostEstimate(
            flops=2 * num_states * rows * width * count * chi,
            bytes_accessed=2 * count * num_states * rows * chi,
            transcendentals=0,
        ),
        name="applied_part",
    )(places, *operands)


def cuts(size):
    middle = max((size - 1) * 5 // 13, 0)
    sizes = [count for count in (size - 1 - middle, middle, 1) if count > 0]
    found, at = [], 0
    for count in sizes:
        found.append((at, count))
        at += count
    return found


def on_device(left_env, right_env, states, mpo):
    num_states, rows, phys, chi = states.shape[1:]
    mw = mpo.shape[0]
    bonds = lax.axis_size("bond")
    paired = bonds == 2
    me = lax.axis_index("bond").astype(jnp.int32)
    places = jnp.stack([me, 1 - me]) if paired else jnp.stack([me, me]) * 0
    scaling = 1.0 / math.sqrt(num_states * chi)
    left = left_env[0].transpose(1, 0, 2)
    right = right_env[0].transpose(1, 0, 2)

    pieces = [(at, passed_along(right[at : at + count], "seg", -1)) for at, count in cuts(mw)]

    wave_split = states[0].transpose(0, 2, 1, 3)
    if paired:
        waves = [wave_split, swapped(wave_split, "bond")]
    else:
        waves = [lax.all_gather(wave_split, "bond", axis=2, tiled=True)]
    here = states[0].reshape(num_states, rows * phys, chi)
    bond_table = mpo.transpose(3, 1, 2, 0).reshape(mw * phys, phys * mw)
    through, *shares = sweep(bond_table, left, waves, here, places, scaling)

    if paired:
        arrived = swapped(shares[1], "bond")
        new_env = shares[0].astype(jnp.float32) + arrived.astype(jnp.float32)
        new_env = new_env.astype(jnp.bfloat16)
    else:
        new_env = lax.psum_scatter(shares[0], "bond", scatter_dimension=1, tiled=True)

    sums = [None, None]
    done = None
    for index, (at, piece) in enumerate(pieces):
        last = index == len(pieces) - 1
        if paired:
            piece = after(piece, through if done is None else done)
            rights = [piece, swapped(piece, "bond")]
        else:
            rights = [lax.all_gather(piece, "bond", axis=1, tiled=True)]
        for part, block in enumerate(rights):
            done = applied_part(through, block, sums[part], at, places, part, phys, last, done)
            if not last:
                sums[part] = done
    return (done[None], new_env.transpose(1, 0, 2)[None])


def solution(mesh):
    in_specs = (
        P("seg", "bond", None, None),
        P("seg", "bond", None, None),
        P("seg", None, "bond", None, None),
        P(),
    )
    out_specs = (P("seg", None, "bond", None, None), P("seg", "bond", None, None))
    return jax.shard_map(
        on_device, mesh=mesh, in_specs=in_specs, out_specs=out_specs, check_vma=False
    )
```

```python
import functools
import math

import jax
import jax.numpy as jnp
from jax import lax
from jax.experimental import pallas as pl
from jax.experimental.pallas import tpu as pltpu
from jax.sharding import PartitionSpec as P

GROUP = 8
MIB = 1 << 20
SWEEP_MIB = 34
ENV_MIB = 34
APPLIED_MIB = 34
ANY = pl.BlockSpec(memory_space=pl.ANY)


def passed_along(array, axis, by):
    size = lax.axis_size(axis)
    pairs = [(i, i + by) for i in range(size) if 0 <= i + by < size]
    return lax.ppermute(array, axis, pairs)


def swapped(array, axis):
    return lax.ppermute(array, axis, [(0, 1), (1, 0)])


def product(left, right, contract):
    return lax.dot_general(left, right, (contract, ((), ())), preferred_element_type=jnp.float32)


def after(array, *others):
    return pl.pallas_call(
        lambda *refs: None,
        in_specs=[ANY] * (1 + len(others)),
        out_specs=ANY,
        out_shape=jax.ShapeDtypeStruct(array.shape, array.dtype),
        input_output_aliases={0: 0},
        compiler_params=pltpu.CompilerParams(vmem_limit_bytes=MIB),
        name="after",
    )(array, *others)


def block_diagonal(bonds, mw, phys):
    size = mw * phys
    full = size * GROUP
    row = lax.broadcasted_iota(jnp.int32, (full, size), 0)
    which = lax.broadcasted_iota(jnp.int32, (full, size), 1)
    pick_row = (row // (GROUP * phys) * phys + row % phys == which).astype(jnp.bfloat16)
    column = lax.broadcasted_iota(jnp.int32, (size, full), 1)
    which = lax.broadcasted_iota(jnp.int32, (size, full), 0)
    pick_column = (column // GROUP == which).astype(jnp.bfloat16)
    spread = product(pick_row, bonds, ((1,), (0,))).astype(jnp.bfloat16)
    spread = product(spread, pick_column, ((1,), (0,)))
    row = lax.broadcasted_iota(jnp.int32, (full, full), 0)
    column = lax.broadcasted_iota(jnp.int32, (full, full), 1)
    same = row % (GROUP * phys) // phys == column % GROUP
    return jnp.where(same, spread, 0.0).astype(jnp.bfloat16)


def sweep_kernel(parts, places, bonds_ref, env_ref, *refs):
    waves, (through_ref, token_ref, lhs, low) = refs[:parts], refs[parts:]
    mw, rows_all, chi_in = env_ref.shape
    num_states, phys, width, chi = waves[0].shape
    part = mw * GROUP
    groups = lhs.shape[0] // part
    rows = groups * GROUP
    table = block_diagonal(bonds_ref[...], mw, phys)
    depth = table.shape[0]
    padded = low.shape[1]
    table = jnp.concatenate([table, jnp.zeros((depth, padded - depth), table.dtype)], axis=1)
    low[:, depth:, :] = jnp.zeros((groups, padded - depth, chi), low.dtype)

    def block(i, _):
        env = env_ref[:, pl.ds(pl.multiple_of(i * rows, rows), rows), :].astype(jnp.float32)
        if parts == 2:
            first, second = env[..., :width], env[..., width:]
            swap = places[0] != 0
            env = jnp.concatenate(
                [jnp.where(swap, second, first), jnp.where(swap, first, second)], axis=2
            )
        env = env.reshape(mw, groups, GROUP, chi_in)
        for g in range(groups):
            lhs[g * part : (g + 1) * part, :] = env[:, g].reshape(part, chi_in).astype(jnp.bfloat16)

        def state(k, _):
            for t in range(phys):
                wave = jnp.concatenate([wave[k, t] for wave in waves], axis=0)
                inner = product(lhs[...], wave, ((1,), (0,))).astype(jnp.bfloat16)
                low[:, t * part : (t + 1) * part, :] = inner.reshape(groups, part, chi)
            for g in range(groups):
                through = product(table, low[g], ((1,), (0,))).astype(jnp.bfloat16)
                size = GROUP * phys
                at = pl.multiple_of(i * rows * phys + g * size, size)
                through_ref[:, k, pl.ds(at, size), :] = through.reshape(mw, size, chi)
            return 0

        lax.fori_loop(0, num_states, state, 0)
        return 0

    lax.fori_loop(0, rows_all // rows, block, 0)
    token_ref[...] = jnp.zeros_like(token_ref)


TOKEN = jax.ShapeDtypeStruct((8, 128), jnp.float32)
WHOLE = pl.BlockSpec(memory_space=pltpu.VMEM)
SCALARS = pl.BlockSpec(memory_space=pltpu.SMEM)


def held_near(array):
    return pltpu.with_memory_space_constraint(array, pltpu.VMEM)


def sweep(bonds, env, waves, places):
    mw, rows_all, chi_in = env.shape
    num_states, phys, _, chi = waves[0].shape
    rows = min(64, rows_all)
    padded = -(-mw * phys * GROUP // 128) * 128
    return pl.pallas_call(
        functools.partial(sweep_kernel, len(waves)),
        in_specs=[SCALARS] + [WHOLE] * (2 + len(waves)),
        out_specs=[WHOLE] * 2,
        scratch_shapes=[
            pltpu.VMEM((mw * rows, chi_in), jnp.bfloat16),
            pltpu.VMEM((rows // GROUP, padded, chi), jnp.bfloat16),
        ],
        out_shape=[
            pltpu.VMEM((mw, num_states, rows_all * phys, chi), jnp.bfloat16),
            TOKEN,
        ],
        compiler_params=pltpu.CompilerParams(vmem_limit_bytes=SWEEP_MIB * MIB),
        cost_estimate=pl.CostEstimate(
            flops=3 * mw * rows_all * chi_in * num_states * phys * chi,
            bytes_accessed=2 * mw * num_states * rows_all * phys * chi,
            transcendentals=0,
        ),
        name="sweep",
    )(places, bonds, env, *waves)


def env_kernel(parts, scaling, places, here_ref, through_ref, *refs):
    outs, turned = refs[:parts], refs[-1]
    num_states, depth, chi = here_ref.shape
    for k in range(num_states):
        turned[:, k * depth : (k + 1) * depth] = here_ref[k].T

    def bond(v, _):
        right = through_ref[v].reshape(num_states * depth, through_ref.shape[3])
        share = (product(turned[...], right, ((1,), (0,))) * scaling).astype(jnp.bfloat16)
        if parts == 2:
            first, second = share[: chi // 2], share[chi // 2 :]
            swap = places[0] != 0
            outs[0][v] = jnp.where(swap, second, first)
            outs[1][v] = jnp.where(swap, first, second)
        else:
            outs[0][v] = share
        return 0

    lax.fori_loop(0, through_ref.shape[0], bond, 0)


def env_shares(here, through, places, parts, scaling):
    mw, num_states, depth, chi = through.shape
    share = jax.ShapeDtypeStruct((mw, chi // parts, chi), jnp.bfloat16)
    return pl.pallas_call(
        functools.partial(env_kernel, parts, scaling),
        in_specs=[SCALARS, WHOLE, WHOLE],
        out_specs=[WHOLE] * (parts + 1),
        input_output_aliases={2: parts},
        scratch_shapes=[pltpu.VMEM((chi, num_states * depth), jnp.bfloat16)],
        out_shape=[share] * parts + [pltpu.VMEM(through.shape, through.dtype)],
        compiler_params=pltpu.CompilerParams(vmem_limit_bytes=ENV_MIB * MIB),
        cost_estimate=pl.CostEstimate(
            flops=2 * mw * num_states * depth * chi * chi,
            bytes_accessed=2 * mw * num_states * depth * chi,
            transcendentals=0,
        ),
        name="env_shares",
    )(places, here, held_near(through))


def applied_kernel(parts, begun, at, phys, places, through_ref, *refs):
    rights, refs = refs[:parts], refs[parts:]
    if begun:
        held_ref, refs = refs[0], refs[1:]
    out_ref, token_ref, turned = refs[0], refs[1], refs[-1]
    last = out_ref.dtype == jnp.bfloat16
    count, chi = rights[0].shape[0], rights[0].shape[2]
    for v in range(count):
        right = jnp.concatenate([right[v] for right in rights], axis=0)
        turned[v * chi : (v + 1) * chi, :] = right.T

    def state(k, _):
        left = jnp.concatenate([through_ref[at + v, k] for v in range(count)], axis=1)
        total = product(left, turned[...], ((1,), (0,)))
        if begun:
            total = total + held_ref[k]
        if last:
            rows, columns = total.shape
            total = total.astype(jnp.bfloat16)
            if parts == 2:
                own, other = total[:, : columns // 2], total[:, columns // 2 :]
                swap = places[0] != 0
                total = jnp.concatenate(
                    [jnp.where(swap, other, own), jnp.where(swap, own, other)], axis=1
                )
            out_ref[k] = total.reshape(rows // phys, phys, columns)
        else:
            out_ref[k] = total
        return 0

    lax.fori_loop(0, through_ref.shape[1], state, 0)
    token_ref[...] = jnp.zeros_like(token_ref)


def applied_part(through, rights, held, at, places, phys, last):
    mw, num_states, rows, chi = through.shape
    count, width, _ = rights[0].shape
    parts = len(rights)
    begun = held is not None
    if last:
        out_shape = jax.ShapeDtypeStruct(
            (num_states, rows // phys, phys, width * parts), jnp.bfloat16
        )
    else:
        out_shape = jax.ShapeDtypeStruct((num_states, rows, width * parts), jnp.float32)
    operands = [held_near(through), *rights] + ([held] if begun else [])
    return pl.pallas_call(
        functools.partial(applied_kernel, parts, begun, at, phys),
        in_specs=[SCALARS] + [WHOLE] * len(operands),
        out_specs=[WHOLE] * (2 if last else 3),
        out_shape=[out_shape, TOKEN]
        + ([] if last else [pltpu.VMEM(through.shape, through.dtype)]),
        input_output_aliases={} if last else {1: 2},
        scratch_shapes=[pltpu.VMEM((count * chi, width * parts), jnp.bfloat16)],
        compiler_params=pltpu.CompilerParams(vmem_limit_bytes=APPLIED_MIB * MIB),
        cost_estimate=pl.CostEstimate(
            flops=2 * num_states * rows * width * parts * count * chi,
            bytes_accessed=2 * count * num_states * rows * chi,
            transcendentals=0,
        ),
        name="applied_part",
    )(places, *operands)


def cuts(size):
    middle = max((size - 1) * 5 // 13, 0)
    sizes = [count for count in (size - 1 - middle, middle, 1) if count > 0]
    found, at = [], 0
    for count in sizes:
        found.append((at, count))
        at += count
    return found


def on_device(left_env, right_env, states, mpo):
    num_states, rows, phys, chi = states.shape[1:]
    mw = mpo.shape[0]
    bonds = lax.axis_size("bond")
    paired = bonds == 2
    me = lax.axis_index("bond").astype(jnp.int32)
    places = jnp.stack([me, 1 - me]) if paired else jnp.stack([me, me]) * 0
    scaling = 1.0 / math.sqrt(num_states * chi)
    left = left_env[0].transpose(1, 0, 2)
    right = right_env[0].transpose(1, 0, 2)

    pieces = [(at, passed_along(right[at : at + count], "seg", -1)) for at, count in cuts(mw)]

    wave_split = states[0].transpose(0, 2, 1, 3)
    if paired:
        waves = [wave_split, swapped(wave_split, "bond")]
    else:
        waves = [lax.all_gather(wave_split, "bond", axis=2, tiled=True)]
    here = states[0].reshape(num_states, rows * phys, chi)
    bond_table = mpo.transpose(3, 1, 2, 0).reshape(mw * phys, phys * mw)
    through, token = sweep(bond_table, left, waves, places)
    *shares, through = env_shares(here, through, places, len(waves), scaling)
    if paired:
        arrived = swapped(shares[1], "bond")
        new_env = shares[0].astype(jnp.float32) + arrived.astype(jnp.float32)
        new_env = new_env.astype(jnp.bfloat16)
    else:
        new_env = lax.psum_scatter(shares[0], "bond", scatter_dimension=1, tiled=True)

    held = None
    for index, (at, piece) in enumerate(pieces):
        if paired:
            piece = after(piece, token)
            rights = [piece, swapped(piece, "bond")]
        else:
            rights = [lax.all_gather(piece, "bond", axis=1, tiled=True)]
        last = index == len(pieces) - 1
        held, token, *rest = applied_part(through, rights, held, at, places, phys, last)
        through = rest[0] if rest else None
    return (held[None], new_env.transpose(1, 0, 2)[None])


def solution(mesh):
    in_specs = (
        P("seg", "bond", None, None),
        P("seg", "bond", None, None),
        P("seg", None, "bond", None, None),
        P(),
    )
    out_specs = (P("seg", None, "bond", None, None), P("seg", "bond", None, None))
    return jax.shard_map(
        on_device, mesh=mesh, in_specs=in_specs, out_specs=out_specs, check_vma=False
    )
```

```python
import functools
import math

import jax
import jax.numpy as jnp
from jax import lax
from jax.experimental import pallas as pl
from jax.experimental.pallas import tpu as pltpu
from jax.sharding import PartitionSpec as P

GROUP = 8
MIB = 1 << 20
SWEEP_MIB = 54
APPLIED_MIB = 40
ANY = pl.BlockSpec(memory_space=pl.ANY)


def passed_along(array, axis, by):
    size = lax.axis_size(axis)
    pairs = [(i, i + by) for i in range(size) if 0 <= i + by < size]
    return lax.ppermute(array, axis, pairs)


def swapped(array, axis):
    return lax.ppermute(array, axis, [(0, 1), (1, 0)])


def product(left, right, contract):
    return lax.dot_general(left, right, (contract, ((), ())), preferred_element_type=jnp.float32)


def after(array, *others):
    return pl.pallas_call(
        lambda *refs: None,
        in_specs=[ANY] * (1 + len(others)),
        out_specs=ANY,
        out_shape=jax.ShapeDtypeStruct(array.shape, array.dtype),
        input_output_aliases={0: 0},
        compiler_params=pltpu.CompilerParams(vmem_limit_bytes=MIB),
        name="after",
    )(array, *others)


def block_diagonal(bonds, mw, phys):
    size = mw * phys
    full = size * GROUP
    row = lax.broadcasted_iota(jnp.int32, (full, size), 0)
    which = lax.broadcasted_iota(jnp.int32, (full, size), 1)
    pick_row = (row // (GROUP * phys) * phys + row % phys == which).astype(jnp.bfloat16)
    column = lax.broadcasted_iota(jnp.int32, (size, full), 1)
    which = lax.broadcasted_iota(jnp.int32, (size, full), 0)
    pick_column = (column // GROUP == which).astype(jnp.bfloat16)
    spread = product(pick_row, bonds, ((1,), (0,))).astype(jnp.bfloat16)
    spread = product(spread, pick_column, ((1,), (0,)))
    row = lax.broadcasted_iota(jnp.int32, (full, full), 0)
    column = lax.broadcasted_iota(jnp.int32, (full, full), 1)
    same = row % (GROUP * phys) // phys == column % GROUP
    return jnp.where(same, spread, 0.0).astype(jnp.bfloat16)


TOKEN = jax.ShapeDtypeStruct((8, 128), jnp.float32)
WHOLE = pl.BlockSpec(memory_space=pltpu.VMEM)
SCALARS = pl.BlockSpec(memory_space=pltpu.SMEM)


def own_first(swap, first, second, axis):
    return jnp.concatenate(
        [jnp.where(swap, second, first), jnp.where(swap, first, second)], axis=axis
    )


def sweep_kernel(parts, pieces, scaling, places, bonds_ref, env_hbm, here_hbm, *refs):
    waves_hbm, refs = refs[:parts], refs[parts:]
    throughs_hbm, refs = refs[:pieces], refs[pieces:]
    token_ref, refs = refs[0], refs[1:]
    outs, refs = refs[:parts], refs[parts:]
    env_ref, here_ref, wave_ref, lhs, low, turned, stage, through_ref = refs[:8]
    env_sems, wave_sems, here_sem, out_sems, through_sems = refs[8:]
    mw, rows_all, chi_in = env_ref.shape
    num_states, phys, _, chi = wave_ref.shape
    width = chi_in // parts
    part = mw * GROUP
    groups = lhs.shape[0] // part
    rows = groups * GROUP
    blocks = rows_all // rows

    def env_copy(i):
        here = pl.ds(pl.multiple_of(i * rows, rows), rows)
        return pltpu.make_async_copy(env_hbm.at[:, here], env_ref.at[:, here], env_sems.at[i])

    def wave_copies(k):
        return [
            pltpu.make_async_copy(
                wave.at[k],
                wave_ref.at[k, :, pl.ds(index * width, width)],
                wave_sems.at[k, index],
            )
            for index, wave in enumerate(waves_hbm)
        ]

    def through_copies(i):
        here = pl.ds(pl.multiple_of(i * rows * phys, rows * phys), rows * phys)
        found, first = [], 0
        for index, out in enumerate(throughs_hbm):
            count = out.shape[0]
            found.append(
                pltpu.make_async_copy(
                    through_ref.at[pl.ds(first, count), :, here],
                    out.at[:, :, here],
                    through_sems.at[i, index],
                )
            )
            first += count
        return found

    here_copy = pltpu.make_async_copy(here_hbm, here_ref, here_sem)
    for n in range(max(blocks, num_states)):
        if n < blocks:
            env_copy(n).start()
        if n < num_states:
            for copy in wave_copies(n):
                copy.start()
    here_copy.start()

    table = block_diagonal(bonds_ref[...], mw, phys)
    depth = table.shape[0]
    padded = low.shape[1]
    table = jnp.concatenate([table, jnp.zeros((depth, padded - depth), table.dtype)], axis=1)
    low[:, depth:, :] = jnp.zeros((groups, padded - depth, chi), low.dtype)
    swap = places[0] != 0

    def block(i, _):
        env_copy(i).wait()
        env = env_ref[:, pl.ds(pl.multiple_of(i * rows, rows), rows), :].astype(jnp.float32)
        if parts == 2:
            env = own_first(swap, env[..., :width], env[..., width:], 2)
        env = env.reshape(mw, groups, GROUP, chi_in)
        for g in range(groups):
            lhs[g * part : (g + 1) * part, :] = env[:, g].reshape(part, chi_in).astype(jnp.bfloat16)

        def state(k, _):
            @pl.when(i == 0)
            def _():
                for copy in wave_copies(k):
                    copy.wait()

            for t in range(phys):
                inner = product(lhs[...], wave_ref[k, t], ((1,), (0,))).astype(jnp.bfloat16)
                low[:, t * part : (t + 1) * part, :] = inner.reshape(groups, part, chi)
            for g in range(groups):
                through = product(table, low[g], ((1,), (0,))).astype(jnp.bfloat16)
                size = GROUP * phys
                at = pl.multiple_of(i * rows * phys + g * size, size)
                through_ref[:, k, pl.ds(at, size), :] = through.reshape(mw, size, chi)
            return 0

        lax.fori_loop(0, num_states, state, 0)
        for copy in through_copies(i):
            copy.start()
        return 0

    lax.fori_loop(0, blocks, block, 0)

    here_copy.wait()
    depth = rows_all * phys
    for k in range(num_states):
        turned[:, k * depth : (k + 1) * depth] = here_ref[k].T

    def out_copies(v, slot):
        return [
            pltpu.make_async_copy(
                stage.at[slot, pl.ds(index * (chi // parts), chi // parts)],
                out.at[v],
                out_sems.at[slot, index],
            )
            for index, out in enumerate(outs)
        ]

    def bond(v, _):
        slot = v % 2
        right = through_ref[v].reshape(num_states * depth, chi)
        share = (product(turned[...], right, ((1,), (0,))) * scaling).astype(jnp.bfloat16)
        if parts == 2:
            share = own_first(swap, share[: chi // 2], share[chi // 2 :], 0)

        @pl.when(v >= 2)
        def _():
            for copy in out_copies(v - 2, slot):
                copy.wait()

        stage[slot] = share
        for copy in out_copies(v, slot):
            copy.start()
        return 0

    lax.fori_loop(0, mw, bond, 0)
    for v in range(max(mw - 2, 0), mw):
        for copy in out_copies(v, v % 2):
            copy.wait()
    for i in range(blocks):
        for copy in through_copies(i):
            copy.wait()
    token_ref[...] = jnp.zeros_like(token_ref)


def sweep(bonds, env, here, waves, places, counts, scaling):
    mw, rows_all, chi_in = env.shape
    num_states, phys, _, chi = waves[0].shape
    rows = min(64, rows_all)
    parts = len(waves)
    padded = -(-mw * phys * GROUP // 128) * 128
    bf16 = jnp.bfloat16
    share = jax.ShapeDtypeStruct((mw, chi // parts, chi), bf16)
    out = pl.pallas_call(
        functools.partial(sweep_kernel, parts, len(counts), scaling),
        in_specs=[SCALARS, WHOLE] + [ANY] * (2 + parts),
        out_specs=[ANY] * len(counts) + [WHOLE] + [ANY] * parts,
        scratch_shapes=[
            pltpu.VMEM(env.shape, bf16),
            pltpu.VMEM(here.shape, bf16),
            pltpu.VMEM((num_states, phys, chi_in, chi), bf16),
            pltpu.VMEM((mw * rows, chi_in), bf16),
            pltpu.VMEM((rows // GROUP, padded, chi), bf16),
            pltpu.VMEM((chi, num_states * rows_all * phys), bf16),
            pltpu.VMEM((2, chi, chi), bf16),
            pltpu.VMEM((mw, num_states, rows_all * phys, chi), bf16),
            pltpu.SemaphoreType.DMA((rows_all // rows,)),
            pltpu.SemaphoreType.DMA((num_states, parts)),
            pltpu.SemaphoreType.DMA,
            pltpu.SemaphoreType.DMA((2, parts)),
            pltpu.SemaphoreType.DMA((rows_all // rows, len(counts))),
        ],
        out_shape=[
            jax.ShapeDtypeStruct((count, num_states, rows_all * phys, chi), bf16)
            for count in counts
        ]
        + [TOKEN]
        + [share] * parts,
        compiler_params=pltpu.CompilerParams(vmem_limit_bytes=SWEEP_MIB * MIB),
        cost_estimate=pl.CostEstimate(
            flops=5 * mw * rows_all * chi_in * num_states * phys * chi,
            bytes_accessed=2 * mw * num_states * rows_all * phys * chi,
            transcendentals=0,
        ),
        name="sweep",
    )(places, bonds, env, here, *waves)
    pieces = len(counts)
    return out[:pieces], out[pieces], out[pieces + 1 :]


def applied_kernel(parts, begun, places, through_hbm, *refs):
    rights_hbm, refs = refs[:parts], refs[parts:]
    if begun:
        held_hbm, refs = refs[0], refs[1:]
    out_hbm, token_ref, through_ref, rights, turned, results = refs[:6]
    through_sems, right_sems, out_sems = refs[6:9]
    if begun:
        held, held_sems = refs[9:]
    last = out_hbm.dtype == jnp.bfloat16
    count, num_states, rows, chi = through_hbm.shape
    width = rights_hbm[0].shape[1]

    def right_copies(v):
        return [
            pltpu.make_async_copy(
                right.at[v], rights.at[v, pl.ds(index * width, width)], right_sems.at[v, index]
            )
            for index, right in enumerate(rights_hbm)
        ]

    def through_copies(k):
        return [
            pltpu.make_async_copy(through_hbm.at[v, k], through_ref.at[v, k], through_sems.at[v, k])
            for v in range(count)
        ]

    def held_copy(k):
        return pltpu.make_async_copy(held_hbm.at[k], held.at[k], held_sems.at[k])

    def out_copy(k, slot):
        return pltpu.make_async_copy(results.at[slot], out_hbm.at[k], out_sems.at[slot])

    for v in range(count):
        for copy in right_copies(v):
            copy.start()
    for k in range(num_states):
        for copy in through_copies(k):
            copy.start()
        if begun:
            held_copy(k).start()
    for v in range(count):
        for copy in right_copies(v):
            copy.wait()
        turned[v * chi : (v + 1) * chi, :] = rights[v].T

    def state(k, _):
        for copy in through_copies(k):
            copy.wait()
        left = jnp.concatenate([through_ref[v, k] for v in range(count)], axis=1)
        total = product(left, turned[...], ((1,), (0,)))
        if begun:
            held_copy(k).wait()
            total = total + held[k]
        if last:
            columns = total.shape[1]
            phys = results.shape[2]
            total = total.astype(jnp.bfloat16)
            if parts == 2:
                swap = places[0] != 0
                total = own_first(swap, total[:, : columns // 2], total[:, columns // 2 :], 1)
            total = total.reshape(rows // phys, phys, columns)
        slot = k % 2

        @pl.when(k >= 2)
        def _():
            out_copy(k - 2, slot).wait()

        results[slot] = total
        out_copy(k, slot).start()
        return 0

    lax.fori_loop(0, num_states, state, 0)
    for k in range(max(num_states - 2, 0), num_states):
        out_copy(k, k % 2).wait()
    token_ref[...] = jnp.zeros_like(token_ref)


def applied_part(through, rights, held, places, phys, last):
    count, num_states, rows, chi = through.shape
    width = rights[0].shape[1]
    parts = len(rights)
    begun = held is not None
    columns = width * parts
    if last:
        out_shape = jax.ShapeDtypeStruct((num_states, rows // phys, phys, columns), jnp.bfloat16)
    else:
        out_shape = jax.ShapeDtypeStruct((num_states, rows, columns), jnp.float32)
    operands = [through, *rights] + ([held] if begun else [])
    return pl.pallas_call(
        functools.partial(applied_kernel, parts, begun),
        in_specs=[SCALARS] + [ANY] * len(operands),
        out_specs=[ANY, WHOLE],
        out_shape=[out_shape, TOKEN],
        scratch_shapes=[
            pltpu.VMEM(through.shape, jnp.bfloat16),
            pltpu.VMEM((count, columns, chi), jnp.bfloat16),
            pltpu.VMEM((count * chi, columns), jnp.bfloat16),
            pltpu.VMEM((2,) + out_shape.shape[1:], out_shape.dtype),
            pltpu.SemaphoreType.DMA((count, num_states)),
            pltpu.SemaphoreType.DMA((count, parts)),
            pltpu.SemaphoreType.DMA((2,)),
        ]
        + (
            [
                pltpu.VMEM((num_states, rows, columns), jnp.float32),
                pltpu.SemaphoreType.DMA((num_states,)),
            ]
            if begun
            else []
        ),
        compiler_params=pltpu.CompilerParams(vmem_limit_bytes=APPLIED_MIB * MIB),
        cost_estimate=pl.CostEstimate(
            flops=2 * num_states * rows * columns * count * chi,
            bytes_accessed=2 * count * num_states * rows * chi,
            transcendentals=0,
        ),
        name="applied_part",
    )(places, *operands)


def cuts(size):
    middle = max((size - 1) * 5 // 13, 0)
    sizes = [count for count in (size - 1 - middle, middle, 1) if count > 0]
    found, at = [], 0
    for count in sizes:
        found.append((at, count))
        at += count
    return found


def on_device(left_env, right_env, states, mpo):
    num_states, rows, phys, chi = states.shape[1:]
    mw = mpo.shape[0]
    bonds = lax.axis_size("bond")
    paired = bonds == 2
    me = lax.axis_index("bond").astype(jnp.int32)
    places = jnp.stack([me, 1 - me]) if paired else jnp.stack([me, me]) * 0
    scaling = 1.0 / math.sqrt(num_states * chi)
    left = left_env[0].transpose(1, 0, 2)
    right = right_env[0].transpose(1, 0, 2)

    starts = cuts(mw)
    pieces = [passed_along(right[at : at + count], "seg", -1) for at, count in starts]

    wave_split = states[0].transpose(0, 2, 1, 3)
    if paired:
        waves = [wave_split, swapped(wave_split, "bond")]
    else:
        waves = [lax.all_gather(wave_split, "bond", axis=2, tiled=True)]
    here = states[0].reshape(num_states, rows * phys, chi)
    bond_table = mpo.transpose(3, 1, 2, 0).reshape(mw * phys, phys * mw)
    counts = [count for _, count in starts]
    throughs, token, shares = sweep(bond_table, left, here, waves, places, counts, scaling)
    if paired:
        arrived = swapped(shares[1], "bond")
        new_env = shares[0].astype(jnp.float32) + arrived.astype(jnp.float32)
        new_env = new_env.astype(jnp.bfloat16)
    else:
        new_env = lax.psum_scatter(shares[0], "bond", scatter_dimension=1, tiled=True)

    held = None
    for index, (through, piece) in enumerate(zip(throughs, pieces)):
        if paired:
            piece = after(piece, token)
            rights = [piece, swapped(piece, "bond")]
        else:
            rights = [lax.all_gather(piece, "bond", axis=1, tiled=True)]
        last = index == len(pieces) - 1
        held, token = applied_part(through, rights, held, places, phys, last)
    return (held[None], new_env.transpose(1, 0, 2)[None])


def solution(mesh):
    in_specs = (
        P("seg", "bond", None, None),
        P("seg", "bond", None, None),
        P("seg", None, "bond", None, None),
        P(),
    )
    out_specs = (P("seg", None, "bond", None, None), P("seg", "bond", None, None))
    return jax.shard_map(
        on_device, mesh=mesh, in_specs=in_specs, out_specs=out_specs, check_vma=False
    )
```

```python
import functools
import math

import jax
import jax.numpy as jnp
from jax import lax
from jax.experimental import pallas as pl
from jax.experimental.pallas import tpu as pltpu
from jax.sharding import PartitionSpec as P

GROUP = 8
MIB = 1 << 20
SWEEP_MIB = 54
ANY = pl.BlockSpec(memory_space=pl.ANY)
TOKEN = pltpu.VMEM((8, 128), jnp.float32)
WHOLE = pl.BlockSpec(memory_space=pltpu.VMEM)
SCALARS = pl.BlockSpec(memory_space=pltpu.SMEM)


def passed_along(array, axis, by):
    size = lax.axis_size(axis)
    pairs = [(i, i + by) for i in range(size) if 0 <= i + by < size]
    return lax.ppermute(array, axis, pairs)


def swapped(array, axis):
    return lax.ppermute(array, axis, [(0, 1), (1, 0)])


def product(left, right, contract):
    return lax.dot_general(left, right, (contract, ((), ())), preferred_element_type=jnp.float32)


def near(array):
    return pltpu.with_memory_space_constraint(array, pltpu.VMEM)


def after(array, token):
    return pl.pallas_call(
        lambda *refs: None,
        in_specs=[ANY, WHOLE],
        out_specs=ANY,
        out_shape=jax.ShapeDtypeStruct(array.shape, array.dtype),
        input_output_aliases={0: 0},
        compiler_params=pltpu.CompilerParams(vmem_limit_bytes=MIB),
        name="after",
    )(array, near(token))


def block_diagonal(bonds, mw, phys):
    size = mw * phys
    full = size * GROUP
    row = lax.broadcasted_iota(jnp.int32, (full, size), 0)
    which = lax.broadcasted_iota(jnp.int32, (full, size), 1)
    pick_row = (row // (GROUP * phys) * phys + row % phys == which).astype(jnp.bfloat16)
    column = lax.broadcasted_iota(jnp.int32, (size, full), 1)
    which = lax.broadcasted_iota(jnp.int32, (size, full), 0)
    pick_column = (column // GROUP == which).astype(jnp.bfloat16)
    spread = product(pick_row, bonds, ((1,), (0,))).astype(jnp.bfloat16)
    spread = product(spread, pick_column, ((1,), (0,)))
    row = lax.broadcasted_iota(jnp.int32, (full, full), 0)
    column = lax.broadcasted_iota(jnp.int32, (full, full), 1)
    same = row % (GROUP * phys) // phys == column % GROUP
    return jnp.where(same, spread, 0.0).astype(jnp.bfloat16)


def own_first(swap, first, second, axis):
    return jnp.concatenate(
        [jnp.where(swap, second, first), jnp.where(swap, first, second)], axis=axis
    )


def sweep_kernel(parts, pieces, scaling, places, bonds_ref, env_hbm, here_hbm, *refs):
    waves_hbm, refs = refs[:parts], refs[parts:]
    throughs_hbm, refs = refs[:pieces], refs[pieces:]
    token_ref, refs = refs[0], refs[1:]
    outs, refs = refs[:parts], refs[parts:]
    env_ref, here_ref, wave_ref, lhs, low, turned, stage, through_ref = refs[:8]
    env_sems, wave_sems, here_sem, out_sems, through_sems = refs[8:]
    mw, rows_all, chi_in = env_ref.shape
    num_states, phys, _, chi = wave_ref.shape
    width = chi_in // parts
    part = mw * GROUP
    groups = lhs.shape[0] // part
    rows = groups * GROUP
    blocks = rows_all // rows

    def env_copy(i):
        here = pl.ds(pl.multiple_of(i * rows, rows), rows)
        return pltpu.make_async_copy(env_hbm.at[:, here], env_ref.at[:, here], env_sems.at[i])

    def wave_copies(k):
        return [
            pltpu.make_async_copy(
                wave.at[k],
                wave_ref.at[k, :, pl.ds(index * width, width)],
                wave_sems.at[k, index],
            )
            for index, wave in enumerate(waves_hbm)
        ]

    def through_copies(i):
        here = pl.ds(pl.multiple_of(i * rows * phys, rows * phys), rows * phys)
        found, first = [], 0
        for index, out in enumerate(throughs_hbm):
            count = out.shape[0]
            found.append(
                pltpu.make_async_copy(
                    through_ref.at[pl.ds(first, count), :, here],
                    out.at[:, :, here],
                    through_sems.at[i, index],
                )
            )
            first += count
        return found

    here_copy = pltpu.make_async_copy(here_hbm.at[0], here_ref, here_sem)
    for n in range(max(blocks, num_states)):
        if n < blocks:
            env_copy(n).start()
        if n < num_states:
            for copy in wave_copies(n):
                copy.start()
    here_copy.start()

    table = block_diagonal(bonds_ref[...], mw, phys)
    depth = table.shape[0]
    padded = low.shape[1]
    table = jnp.concatenate([table, jnp.zeros((depth, padded - depth), table.dtype)], axis=1)
    low[:, depth:, :] = jnp.zeros((groups, padded - depth, chi), low.dtype)
    swap = places[0] != 0

    def block(i, _):
        env_copy(i).wait()
        env = env_ref[:, pl.ds(pl.multiple_of(i * rows, rows), rows), :].astype(jnp.float32)
        if parts == 2:
            env = own_first(swap, env[..., :width], env[..., width:], 2)
        env = env.reshape(mw, groups, GROUP, chi_in)
        for g in range(groups):
            lhs[g * part : (g + 1) * part, :] = env[:, g].reshape(part, chi_in).astype(jnp.bfloat16)

        def state(k, _):
            @pl.when(i == 0)
            def _():
                for copy in wave_copies(k):
                    copy.wait()

                @pl.when(k == 0)
                def _():
                    here_copy.wait()

            here = here_ref[k, pl.ds(pl.multiple_of(i * rows, rows), rows)]
            at = pl.multiple_of((k * blocks + i) * rows * phys, rows * phys)
            turned[:, pl.ds(at, rows * phys)] = here.reshape(rows * phys, chi).T
            for t in range(phys):
                inner = product(lhs[...], wave_ref[k, t], ((1,), (0,))).astype(jnp.bfloat16)
                low[:, t * part : (t + 1) * part, :] = inner.reshape(groups, part, chi)
            for g in range(groups):
                through = product(table, low[g], ((1,), (0,))).astype(jnp.bfloat16)
                size = GROUP * phys
                at = pl.multiple_of(i * rows * phys + g * size, size)
                through_ref[:, k, pl.ds(at, size), :] = through.reshape(mw, size, chi)
            return 0

        lax.fori_loop(0, num_states, state, 0)
        for copy in through_copies(i):
            copy.start()
        return 0

    lax.fori_loop(0, blocks, block, 0)

    depth = rows_all * phys

    def out_copies(v, slot):
        return [
            pltpu.make_async_copy(
                stage.at[slot, pl.ds(index * (chi // parts), chi // parts)],
                out.at[v],
                out_sems.at[slot, index],
            )
            for index, out in enumerate(outs)
        ]

    def bond(v, _):
        slot = v % 2
        right = through_ref[v].reshape(num_states * depth, chi)
        share = (product(turned[...], right, ((1,), (0,))) * scaling).astype(jnp.bfloat16)
        if parts == 2:
            share = own_first(swap, share[: chi // 2], share[chi // 2 :], 0)

        @pl.when(v >= 2)
        def _():
            for copy in out_copies(v - 2, slot):
                copy.wait()

        stage[slot] = share
        for copy in out_copies(v, slot):
            copy.start()
        return 0

    lax.fori_loop(0, mw, bond, 0)
    for v in range(max(mw - 2, 0), mw):
        for copy in out_copies(v, v % 2):
            copy.wait()
    for i in range(blocks):
        for copy in through_copies(i):
            copy.wait()
    token_ref[...] = jnp.zeros_like(token_ref)


def sweep(bonds, env, here, waves, places, counts, scaling):
    mw, rows_all, chi_in = env.shape
    num_states, phys, _, chi = waves[0].shape
    rows = min(64, rows_all)
    parts = len(waves)
    padded = -(-mw * phys * GROUP // 128) * 128
    bf16 = jnp.bfloat16
    share = jax.ShapeDtypeStruct((mw, chi // parts, chi), bf16)
    out = pl.pallas_call(
        functools.partial(sweep_kernel, parts, len(counts), scaling),
        in_specs=[SCALARS, WHOLE] + [ANY] * (2 + parts),
        out_specs=[ANY] * len(counts) + [WHOLE] + [ANY] * parts,
        scratch_shapes=[
            pltpu.VMEM(env.shape, bf16),
            pltpu.VMEM(here.shape[1:], bf16),
            pltpu.VMEM((num_states, phys, chi_in, chi), bf16),
            pltpu.VMEM((mw * rows, chi_in), bf16),
            pltpu.VMEM((rows // GROUP, padded, chi), bf16),
            pltpu.VMEM((chi, num_states * rows_all * phys), bf16),
            pltpu.VMEM((2, chi, chi), bf16),
            pltpu.VMEM((mw, num_states, rows_all * phys, chi), bf16),
            pltpu.SemaphoreType.DMA((rows_all // rows,)),
            pltpu.SemaphoreType.DMA((num_states, parts)),
            pltpu.SemaphoreType.DMA,
            pltpu.SemaphoreType.DMA((2, parts)),
            pltpu.SemaphoreType.DMA((rows_all // rows, len(counts))),
        ],
        out_shape=[
            jax.ShapeDtypeStruct((count, num_states, rows_all * phys, chi), bf16)
            for count in counts
        ]
        + [TOKEN]
        + [share] * parts,
        compiler_params=pltpu.CompilerParams(vmem_limit_bytes=SWEEP_MIB * MIB),
        cost_estimate=pl.CostEstimate(
            flops=5 * mw * rows_all * chi_in * num_states * phys * chi,
            bytes_accessed=2 * mw * num_states * rows_all * phys * chi,
            transcendentals=0,
        ),
        name="sweep",
    )(places, bonds, env, here, *waves)
    pieces = len(counts)
    return out[:pieces], out[pieces], out[pieces + 1 :]


def applied_kernel(parts, begun, close, places, through_in, *refs):
    rights, refs = refs[:parts], refs[parts:]
    if begun:
        held, refs = refs[0], refs[1:]
    out, token_ref, turned, refs = refs[0], refs[1], refs[2], refs[3:]
    last = out.dtype == jnp.bfloat16
    count, num_states, rows, chi = through_in.shape
    if last:
        results, out_sems, refs = refs[0], refs[1], refs[2:]
    if close:
        through_ref = through_in
    else:
        through_ref, through_sems = refs

    def through_copies(k):
        return [
            pltpu.make_async_copy(through_in.at[v, k], through_ref.at[v, k], through_sems.at[v, k])
            for v in range(count)
        ]

    def out_copy(k, slot):
        return pltpu.make_async_copy(results.at[slot], out.at[k], out_sems.at[slot])

    if not close:
        for k in range(num_states):
            for copy in through_copies(k):
                copy.start()
    for v in range(count):
        right = jnp.concatenate([right[v] for right in rights], axis=0)
        turned[v * chi : (v + 1) * chi, :] = right.T

    def state(k, _):
        if not close:
            for copy in through_copies(k):
                copy.wait()
        left = jnp.concatenate([through_ref[v, k] for v in range(count)], axis=1)
        total = product(left, turned[...], ((1,), (0,)))
        if begun:
            total = total + held[k]
        if not last:
            out[k] = total
            return 0
        columns = total.shape[1]
        phys = results.shape[2]
        total = total.astype(jnp.bfloat16)
        if parts == 2:
            swap = places[0] != 0
            total = own_first(swap, total[:, : columns // 2], total[:, columns // 2 :], 1)
        slot = k % 2

        @pl.when(k >= 2)
        def _():
            out_copy(k - 2, slot).wait()

        results[slot] = total.reshape(rows // phys, phys, columns)
        out_copy(k, slot).start()
        return 0

    lax.fori_loop(0, num_states, state, 0)
    if last:
        for k in range(max(num_states - 2, 0), num_states):
            out_copy(k, k % 2).wait()
    token_ref[...] = jnp.zeros_like(token_ref)


def applied_part(through, rights, held, places, phys, last):
    count, num_states, rows, chi = through.shape
    width = rights[0].shape[1]
    parts = len(rights)
    begun = held is not None
    close = count <= 4
    columns = width * parts
    scratch = [pltpu.VMEM((count * chi, columns), jnp.bfloat16)]
    if last:
        shape = (num_states, rows // phys, phys, columns)
        out_shape, out_spec = jax.ShapeDtypeStruct(shape, jnp.bfloat16), ANY
        scratch += [pltpu.VMEM((2,) + shape[1:], jnp.bfloat16), pltpu.SemaphoreType.DMA((2,))]
    else:
        out_shape, out_spec = pltpu.VMEM((num_states, rows, columns), jnp.float32), WHOLE
    if not close:
        scratch += [
            pltpu.VMEM(through.shape, jnp.bfloat16),
            pltpu.SemaphoreType.DMA((count, num_states)),
        ]
    operands = [near(through) if close else through]
    operands += [near(right) for right in rights] + ([near(held)] if begun else [])
    return pl.pallas_call(
        functools.partial(applied_kernel, parts, begun, close),
        in_specs=[SCALARS, WHOLE if close else ANY] + [WHOLE] * (len(operands) - 1),
        out_specs=[out_spec, WHOLE],
        out_shape=[out_shape, TOKEN],
        scratch_shapes=scratch,
        compiler_params=pltpu.CompilerParams(vmem_limit_bytes=(16 if close else 34) * MIB),
        cost_estimate=pl.CostEstimate(
            flops=2 * num_states * rows * columns * count * chi,
            bytes_accessed=2 * count * num_states * rows * chi,
            transcendentals=0,
        ),
        name="applied_part",
    )(places, *operands)


def cuts(size):
    middle = max((size - 1) * 3 // 13, 0)
    sizes = [count for count in (size - 1 - middle, middle, 1) if count > 0]
    found, at = [], 0
    for count in sizes:
        found.append((at, count))
        at += count
    return found


def on_device(left_env, right_env, states, mpo):
    num_states, rows, phys, chi = states.shape[1:]
    mw = mpo.shape[0]
    bonds = lax.axis_size("bond")
    paired = bonds == 2
    me = lax.axis_index("bond").astype(jnp.int32)
    places = jnp.stack([me, 1 - me]) if paired else jnp.stack([me, me]) * 0
    scaling = 1.0 / math.sqrt(num_states * chi)
    left = left_env[0].transpose(1, 0, 2)
    right = right_env[0].transpose(1, 0, 2)

    starts = cuts(mw)
    pieces = [passed_along(right[at : at + count], "seg", -1) for at, count in starts]

    wave_split = states[0].transpose(0, 2, 1, 3)
    if paired:
        waves = [wave_split, swapped(wave_split, "bond")]
    else:
        waves = [lax.all_gather(wave_split, "bond", axis=2, tiled=True)]
    bond_table = mpo.transpose(3, 1, 2, 0).reshape(mw * phys, phys * mw)
    counts = [count for _, count in starts]
    throughs, token, shares = sweep(bond_table, left, states, waves, places, counts, scaling)
    if paired:
        arrived = swapped(shares[1], "bond")
        new_env = shares[0].astype(jnp.float32) + arrived.astype(jnp.float32)
        new_env = new_env.astype(jnp.bfloat16)
    else:
        new_env = lax.psum_scatter(shares[0], "bond", scatter_dimension=1, tiled=True)

    held = None
    for index, (through, piece) in enumerate(zip(throughs, pieces)):
        if paired:
            piece = after(piece, token)
            rights = [piece, swapped(piece, "bond")]
        else:
            rights = [lax.all_gather(piece, "bond", axis=1, tiled=True)]
        last = index == len(pieces) - 1
        held, token = applied_part(through, rights, held, places, phys, last)
    return (held[None], new_env.transpose(1, 0, 2)[None])


def solution(mesh):
    in_specs = (
        P("seg", "bond", None, None),
        P("seg", "bond", None, None),
        P("seg", None, "bond", None, None),
        P(),
    )
    out_specs = (P("seg", None, "bond", None, None), P("seg", "bond", None, None))
    return jax.shard_map(
        on_device, mesh=mesh, in_specs=in_specs, out_specs=out_specs, check_vma=False
    )
```

```python
import functools
import math

import jax
import jax.numpy as jnp
from jax import lax
from jax.experimental import pallas as pl
from jax.experimental.pallas import tpu as pltpu
from jax.sharding import PartitionSpec as P

GROUP = 8
MIB = 1 << 20
SWEEP_MIB = 54
ANY = pl.BlockSpec(memory_space=pl.ANY)
TOKEN = pltpu.VMEM((8, 128), jnp.float32)
WHOLE = pl.BlockSpec(memory_space=pltpu.VMEM)
SCALARS = pl.BlockSpec(memory_space=pltpu.SMEM)


def passed_along(array, axis, by):
    size = lax.axis_size(axis)
    pairs = [(i, i + by) for i in range(size) if 0 <= i + by < size]
    return lax.ppermute(array, axis, pairs)


def swapped(array, axis):
    return lax.ppermute(array, axis, [(0, 1), (1, 0)])


def product(left, right, contract):
    return lax.dot_general(left, right, (contract, ((), ())), preferred_element_type=jnp.float32)


def near(array):
    return pltpu.with_memory_space_constraint(array, pltpu.VMEM)


def far(array):
    return pltpu.with_memory_space_constraint(array, pltpu.HBM)


def after(array, token):
    return pl.pallas_call(
        lambda *refs: None,
        in_specs=[ANY, WHOLE],
        out_specs=ANY,
        out_shape=jax.ShapeDtypeStruct(array.shape, array.dtype),
        input_output_aliases={0: 0},
        compiler_params=pltpu.CompilerParams(vmem_limit_bytes=MIB),
        name="after",
    )(array, near(token))


def block_diagonal(bonds, mw, phys):
    size = mw * phys
    full = size * GROUP
    row = lax.broadcasted_iota(jnp.int32, (full, size), 0)
    which = lax.broadcasted_iota(jnp.int32, (full, size), 1)
    pick_row = (row // (GROUP * phys) * phys + row % phys == which).astype(jnp.bfloat16)
    column = lax.broadcasted_iota(jnp.int32, (size, full), 1)
    which = lax.broadcasted_iota(jnp.int32, (size, full), 0)
    pick_column = (column // GROUP == which).astype(jnp.bfloat16)
    spread = product(pick_row, bonds, ((1,), (0,))).astype(jnp.bfloat16)
    spread = product(spread, pick_column, ((1,), (0,)))
    row = lax.broadcasted_iota(jnp.int32, (full, full), 0)
    column = lax.broadcasted_iota(jnp.int32, (full, full), 1)
    same = row % (GROUP * phys) // phys == column % GROUP
    return jnp.where(same, spread, 0.0).astype(jnp.bfloat16)


def own_first(swap, first, second, axis):
    return jnp.concatenate(
        [jnp.where(swap, second, first), jnp.where(swap, first, second)], axis=axis
    )


def sweep_kernel(parts, pieces, scaling, places, bonds_ref, env_hbm, here_hbm, *refs):
    waves_hbm, refs = refs[:parts], refs[parts:]
    throughs_hbm, refs = refs[:pieces], refs[pieces:]
    token_ref, refs = refs[0], refs[1:]
    outs, refs = refs[:parts], refs[parts:]
    env_ref, here_ref, wave_ref, lhs, low, turned, stage, through_ref = refs[:8]
    env_sems, wave_sems, here_sem, out_sems, through_sems = refs[8:]
    mw, rows_all, chi_in = env_ref.shape
    num_states, phys, _, chi = wave_ref.shape
    width = chi_in // parts
    part = mw * GROUP
    groups = lhs.shape[0] // part
    rows = groups * GROUP
    blocks = rows_all // rows

    def env_copy(i):
        here = pl.ds(pl.multiple_of(i * rows, rows), rows)
        return pltpu.make_async_copy(env_hbm.at[:, here], env_ref.at[:, here], env_sems.at[i])

    def wave_copies(k):
        return [
            pltpu.make_async_copy(
                wave.at[k],
                wave_ref.at[k, :, pl.ds(index * width, width)],
                wave_sems.at[k, index],
            )
            for index, wave in enumerate(waves_hbm)
        ]

    def through_copies(i):
        here = pl.ds(pl.multiple_of(i * rows * phys, rows * phys), rows * phys)
        found, first = [], 0
        for index, out in enumerate(throughs_hbm):
            count = out.shape[0]
            found.append(
                pltpu.make_async_copy(
                    through_ref.at[pl.ds(first, count), :, here],
                    out.at[:, :, here],
                    through_sems.at[i, index],
                )
            )
            first += count
        return found

    here_copy = pltpu.make_async_copy(here_hbm.at[0], here_ref, here_sem)
    for n in range(max(blocks, num_states)):
        if n < blocks:
            env_copy(n).start()
        if n < num_states:
            for copy in wave_copies(n):
                copy.start()
    here_copy.start()

    table = block_diagonal(bonds_ref[...], mw, phys)
    depth = table.shape[0]
    padded = low.shape[1]
    table = jnp.concatenate([table, jnp.zeros((depth, padded - depth), table.dtype)], axis=1)
    low[:, depth:, :] = jnp.zeros((groups, padded - depth, chi), low.dtype)
    swap = places[0] != 0

    def block(i, _):
        env_copy(i).wait()
        env = env_ref[:, pl.ds(pl.multiple_of(i * rows, rows), rows), :].astype(jnp.float32)
        if parts == 2:
            env = own_first(swap, env[..., :width], env[..., width:], 2)
        env = env.reshape(mw, groups, GROUP, chi_in)
        for g in range(groups):
            lhs[g * part : (g + 1) * part, :] = env[:, g].reshape(part, chi_in).astype(jnp.bfloat16)

        def state(k, _):
            @pl.when(i == 0)
            def _():
                for copy in wave_copies(k):
                    copy.wait()

                @pl.when(k == 0)
                def _():
                    here_copy.wait()

            here = here_ref[k, pl.ds(pl.multiple_of(i * rows, rows), rows)]
            at = pl.multiple_of((k * blocks + i) * rows * phys, rows * phys)
            turned[:, pl.ds(at, rows * phys)] = here.reshape(rows * phys, chi).T
            for t in range(phys):
                inner = product(lhs[...], wave_ref[k, t], ((1,), (0,))).astype(jnp.bfloat16)
                low[:, t * part : (t + 1) * part, :] = inner.reshape(groups, part, chi)
            for g in range(groups):
                through = product(table, low[g], ((1,), (0,))).astype(jnp.bfloat16)
                size = GROUP * phys
                at = pl.multiple_of(i * rows * phys + g * size, size)
                through_ref[:, k, pl.ds(at, size), :] = through.reshape(mw, size, chi)
            return 0

        lax.fori_loop(0, num_states, state, 0)
        for copy in through_copies(i):
            copy.start()
        return 0

    lax.fori_loop(0, blocks, block, 0)

    depth = rows_all * phys

    def out_copies(v, slot):
        return [
            pltpu.make_async_copy(
                stage.at[slot, pl.ds(index * (chi // parts), chi // parts)],
                out.at[v],
                out_sems.at[slot, index],
            )
            for index, out in enumerate(outs)
        ]

    def bond(v, _):
        slot = v % 2
        right = through_ref[v].reshape(num_states * depth, chi)
        share = (product(turned[...], right, ((1,), (0,))) * scaling).astype(jnp.bfloat16)
        if parts == 2:
            share = own_first(swap, share[: chi // 2], share[chi // 2 :], 0)

        @pl.when(v >= 2)
        def _():
            for copy in out_copies(v - 2, slot):
                copy.wait()

        stage[slot] = share
        for copy in out_copies(v, slot):
            copy.start()
        return 0

    lax.fori_loop(0, mw, bond, 0)
    for v in range(max(mw - 2, 0), mw):
        for copy in out_copies(v, v % 2):
            copy.wait()
    for i in range(blocks):
        for copy in through_copies(i):
            copy.wait()
    token_ref[...] = jnp.zeros_like(token_ref)


def sweep(bonds, env, here, waves, places, counts, scaling):
    mw, rows_all, chi_in = env.shape
    num_states, phys, _, chi = waves[0].shape
    rows = min(64, rows_all)
    parts = len(waves)
    padded = -(-mw * phys * GROUP // 128) * 128
    bf16 = jnp.bfloat16
    share = jax.ShapeDtypeStruct((mw, chi // parts, chi), bf16)
    out = pl.pallas_call(
        functools.partial(sweep_kernel, parts, len(counts), scaling),
        in_specs=[SCALARS, WHOLE] + [ANY] * (2 + parts),
        out_specs=[ANY] * len(counts) + [WHOLE] + [ANY] * parts,
        scratch_shapes=[
            pltpu.VMEM(env.shape, bf16),
            pltpu.VMEM(here.shape[1:], bf16),
            pltpu.VMEM((num_states, phys, chi_in, chi), bf16),
            pltpu.VMEM((mw * rows, chi_in), bf16),
            pltpu.VMEM((rows // GROUP, padded, chi), bf16),
            pltpu.VMEM((chi, num_states * rows_all * phys), bf16),
            pltpu.VMEM((2, chi, chi), bf16),
            pltpu.VMEM((mw, num_states, rows_all * phys, chi), bf16),
            pltpu.SemaphoreType.DMA((rows_all // rows,)),
            pltpu.SemaphoreType.DMA((num_states, parts)),
            pltpu.SemaphoreType.DMA,
            pltpu.SemaphoreType.DMA((2, parts)),
            pltpu.SemaphoreType.DMA((rows_all // rows, len(counts))),
        ],
        out_shape=[
            jax.ShapeDtypeStruct((count, num_states, rows_all * phys, chi), bf16)
            for count in counts
        ]
        + [TOKEN]
        + [share] * parts,
        compiler_params=pltpu.CompilerParams(vmem_limit_bytes=SWEEP_MIB * MIB),
        cost_estimate=pl.CostEstimate(
            flops=5 * mw * rows_all * chi_in * num_states * phys * chi,
            bytes_accessed=2 * mw * num_states * rows_all * phys * chi,
            transcendentals=0,
        ),
        name="sweep",
    )(places, bonds, env, here, *waves)
    pieces = len(counts)
    return out[:pieces], out[pieces], out[pieces + 1 :]


def applied_kernel(parts, pieces, begun, close, places, through_in, *refs):
    rights, refs = refs[: parts * pieces], refs[parts * pieces :]
    if begun:
        held, refs = refs[0], refs[1:]
    out, token_ref, turned, refs = refs[0], refs[1], refs[2], refs[3:]
    last = out.dtype == jnp.bfloat16
    count, num_states, rows, chi = through_in.shape
    if last:
        results, out_sems, refs = refs[0], refs[1], refs[2:]
    if close:
        through_ref = through_in
    else:
        through_ref, through_sems = refs

    def through_copies(k):
        return [
            pltpu.make_async_copy(through_in.at[v, k], through_ref.at[v, k], through_sems.at[v, k])
            for v in range(count)
        ]

    def out_copy(k, slot):
        return pltpu.make_async_copy(results.at[slot], out.at[k], out_sems.at[slot])

    if not close:
        for k in range(num_states):
            for copy in through_copies(k):
                copy.start()
    v = 0
    for piece in range(pieces):
        blocks = rights[piece * parts : (piece + 1) * parts]
        for n in range(blocks[0].shape[0]):
            right = jnp.concatenate([block[n] for block in blocks], axis=0)
            turned[v * chi : (v + 1) * chi, :] = right.T
            v += 1

    def state(k, _):
        if not close:
            for copy in through_copies(k):
                copy.wait()
        left = jnp.concatenate([through_ref[v, k] for v in range(count)], axis=1)
        total = product(left, turned[...], ((1,), (0,)))
        if begun:
            total = total + held[k]
        if not last:
            out[k] = total
            return 0
        columns = total.shape[1]
        phys = results.shape[2]
        total = total.astype(jnp.bfloat16)
        if parts == 2:
            swap = places[0] != 0
            total = own_first(swap, total[:, : columns // 2], total[:, columns // 2 :], 1)
        slot = k % 2

        @pl.when(k >= 2)
        def _():
            out_copy(k - 2, slot).wait()

        results[slot] = total.reshape(rows // phys, phys, columns)
        out_copy(k, slot).start()
        return 0

    lax.fori_loop(0, num_states, state, 0)
    if last:
        for k in range(max(num_states - 2, 0), num_states):
            out_copy(k, k % 2).wait()
    token_ref[...] = jnp.zeros_like(token_ref)


def applied_part(through, rights, held, places, phys, last):
    count, num_states, rows, chi = through.shape
    width = rights[0][0].shape[1]
    parts = len(rights[0])
    begun = held is not None
    close = count <= 4
    columns = width * parts
    scratch = [pltpu.VMEM((count * chi, columns), jnp.bfloat16)]
    if last:
        shape = (num_states, rows // phys, phys, columns)
        out_shape, out_spec = jax.ShapeDtypeStruct(shape, jnp.bfloat16), ANY
        scratch += [pltpu.VMEM((2,) + shape[1:], jnp.bfloat16), pltpu.SemaphoreType.DMA((2,))]
    else:
        out_shape, out_spec = pltpu.VMEM((num_states, rows, columns), jnp.float32), WHOLE
    if not close:
        scratch += [
            pltpu.VMEM(through.shape, jnp.bfloat16),
            pltpu.SemaphoreType.DMA((count, num_states)),
        ]
    operands = [near(through) if close else far(through)]
    operands += [near(block) for blocks in rights for block in blocks] + ([near(held)] if begun else [])
    return pl.pallas_call(
        functools.partial(applied_kernel, parts, len(rights), begun, close),
        in_specs=[SCALARS, WHOLE if close else ANY] + [WHOLE] * (len(operands) - 1),
        out_specs=[out_spec, WHOLE],
        out_shape=[out_shape, TOKEN],
        scratch_shapes=scratch,
        compiler_params=pltpu.CompilerParams(vmem_limit_bytes=(16 if close else 34) * MIB),
        cost_estimate=pl.CostEstimate(
            flops=0,
            bytes_accessed=0,
            transcendentals=0,
        ),
        name="applied_part",
    )(places, *operands)


def cuts(size):
    first = (size - 1) * 6 // 13
    return [[count] for count in (first, size - 1 - first, 1) if count > 0]


def on_device(left_env, right_env, states, mpo):
    num_states, rows, phys, chi = states.shape[1:]
    mw = mpo.shape[0]
    bonds = lax.axis_size("bond")
    paired = bonds == 2
    me = lax.axis_index("bond").astype(jnp.int32)
    places = jnp.stack([me, 1 - me]) if paired else jnp.stack([me, me]) * 0
    scaling = 1.0 / math.sqrt(num_states * chi)
    left = left_env[0].transpose(1, 0, 2)
    right = right_env[0].transpose(1, 0, 2)

    stages = cuts(mw)
    pieces, first = [], 0
    for stage in stages:
        pieces.append([])
        for count in stage:
            piece = passed_along(right[first : first + count], "seg", -1)
            pieces[-1].append(piece)
            first += count

    wave_split = states[0].transpose(0, 2, 1, 3)
    if paired:
        waves = [wave_split, swapped(wave_split, "bond")]
    else:
        waves = [lax.all_gather(wave_split, "bond", axis=2, tiled=True)]
    bond_table = mpo.transpose(3, 1, 2, 0).reshape(mw * phys, phys * mw)
    counts = [sum(stage) for stage in stages]
    throughs, token, shares = sweep(bond_table, left, states, waves, places, counts, scaling)
    if paired:
        arrived = swapped(shares[1], "bond")
        new_env = shares[0].astype(jnp.float32) + arrived.astype(jnp.float32)
        new_env = new_env.astype(jnp.bfloat16)
    else:
        new_env = lax.psum_scatter(shares[0], "bond", scatter_dimension=1, tiled=True)

    held = None
    for index, (through, stage) in enumerate(zip(throughs, pieces)):
        rights = []
        for piece in stage:
            if paired:
                piece = after(piece, token)
                rights.append([piece, swapped(piece, "bond")])
            else:
                rights.append([lax.all_gather(piece, "bond", axis=1, tiled=True)])
        last = index == len(pieces) - 1
        held, token = applied_part(through, rights, held, places, phys, last)
    return (held[None], new_env.transpose(1, 0, 2)[None])


def solution(mesh):
    in_specs = (
        P("seg", "bond", None, None),
        P("seg", "bond", None, None),
        P("seg", None, "bond", None, None),
        P(),
    )
    out_specs = (P("seg", None, "bond", None, None), P("seg", "bond", None, None))
    return jax.shard_map(
        on_device, mesh=mesh, in_specs=in_specs, out_specs=out_specs, check_vma=False
    )
```

```python
import functools
import math

import jax
import jax.numpy as jnp
from jax import lax
from jax.experimental import pallas as pl
from jax.experimental.pallas import tpu as pltpu
from jax.sharding import PartitionSpec as P

GROUP = 8
MIB = 1 << 20
SWEEP_MIB = 54
ANY = pl.BlockSpec(memory_space=pl.ANY)
TOKEN = pltpu.VMEM((8, 128), jnp.float32)
WHOLE = pl.BlockSpec(memory_space=pltpu.VMEM)
SCALARS = pl.BlockSpec(memory_space=pltpu.SMEM)


def passed_along(array, axis, by):
    size = lax.axis_size(axis)
    pairs = [(i, i + by) for i in range(size) if 0 <= i + by < size]
    return lax.ppermute(array, axis, pairs)


def swapped(array, axis):
    return lax.ppermute(array, axis, [(0, 1), (1, 0)])


def product(left, right, contract):
    return lax.dot_general(left, right, (contract, ((), ())), preferred_element_type=jnp.float32)


def near(array):
    return pltpu.with_memory_space_constraint(array, pltpu.VMEM)


def far(array):
    return pltpu.with_memory_space_constraint(array, pltpu.HBM)


def after(array, token):
    return pl.pallas_call(
        lambda *refs: None,
        in_specs=[ANY, WHOLE],
        out_specs=ANY,
        out_shape=jax.ShapeDtypeStruct(array.shape, array.dtype),
        input_output_aliases={0: 0},
        compiler_params=pltpu.CompilerParams(vmem_limit_bytes=MIB),
        name="after",
    )(array, near(token))


def block_diagonal(bonds, mw, phys):
    size = mw * phys
    full = size * GROUP
    row = lax.broadcasted_iota(jnp.int32, (full, size), 0)
    which = lax.broadcasted_iota(jnp.int32, (full, size), 1)
    pick_row = (row // (GROUP * phys) * phys + row % phys == which).astype(jnp.bfloat16)
    column = lax.broadcasted_iota(jnp.int32, (size, full), 1)
    which = lax.broadcasted_iota(jnp.int32, (size, full), 0)
    pick_column = (column // GROUP == which).astype(jnp.bfloat16)
    spread = product(pick_row, bonds, ((1,), (0,))).astype(jnp.bfloat16)
    spread = product(spread, pick_column, ((1,), (0,)))
    row = lax.broadcasted_iota(jnp.int32, (full, full), 0)
    column = lax.broadcasted_iota(jnp.int32, (full, full), 1)
    same = row % (GROUP * phys) // phys == column % GROUP
    return jnp.where(same, spread, 0.0).astype(jnp.bfloat16)


def own_first(swap, first, second, axis):
    return jnp.concatenate(
        [jnp.where(swap, second, first), jnp.where(swap, first, second)], axis=axis
    )


def sweep_kernel(parts, turns, pieces, scaling, places, bonds_ref, env_hbm, here_hbm, *refs):
    waves_hbm, refs = refs[: parts * turns], refs[parts * turns :]
    throughs_hbm, refs = refs[:pieces], refs[pieces:]
    token_ref, refs = refs[0], refs[1:]
    outs, refs = refs[:parts], refs[parts:]
    env_ref, here_ref, wave_ref, lhs, low, turned, stage, through_ref = refs[:8]
    env_sems, wave_sems, here_sem, out_sems, through_sems = refs[8:]
    mw, rows_all, chi_in = env_ref.shape
    num_states, phys, _, chi = wave_ref.shape
    width = chi_in // parts
    part = mw * GROUP
    groups = lhs.shape[0] // part
    rows = groups * GROUP
    blocks = rows_all // rows

    def env_copy(i):
        here = pl.ds(pl.multiple_of(i * rows, rows), rows)
        return pltpu.make_async_copy(env_hbm.at[:, here], env_ref.at[:, here], env_sems.at[i])

    def wave_starts(k):
        turn, inside = divmod(k, waves_hbm[0].shape[0])
        return [
            pltpu.make_async_copy(
                waves_hbm[turn * parts + index].at[inside],
                wave_ref.at[k, :, pl.ds(index * width, width)],
                wave_sems.at[k, index],
            )
            for index in range(parts)
        ]

    def wave_copies(k):
        return [
            pltpu.make_async_copy(
                waves_hbm[index].at[0],
                wave_ref.at[k, :, pl.ds(index * width, width)],
                wave_sems.at[k, index],
            )
            for index in range(parts)
        ]

    def through_copies(i):
        here = pl.ds(pl.multiple_of(i * rows * phys, rows * phys), rows * phys)
        found, first = [], 0
        for index, out in enumerate(throughs_hbm):
            count = out.shape[0]
            found.append(
                pltpu.make_async_copy(
                    through_ref.at[pl.ds(first, count), :, here],
                    out.at[:, :, here],
                    through_sems.at[i, index],
                )
            )
            first += count
        return found

    here_copy = pltpu.make_async_copy(here_hbm.at[0], here_ref, here_sem)
    for n in range(max(blocks, num_states)):
        if n < blocks:
            env_copy(n).start()
        if n < num_states:
            for copy in wave_starts(n):
                copy.start()
    here_copy.start()

    table = block_diagonal(bonds_ref[...], mw, phys)
    depth = table.shape[0]
    padded = low.shape[1]
    table = jnp.concatenate([table, jnp.zeros((depth, padded - depth), table.dtype)], axis=1)
    low[:, depth:, :] = jnp.zeros((groups, padded - depth, chi), low.dtype)
    swap = places[0] != 0

    def block(i, _):
        env_copy(i).wait()
        env = env_ref[:, pl.ds(pl.multiple_of(i * rows, rows), rows), :].astype(jnp.float32)
        if parts == 2:
            env = own_first(swap, env[..., :width], env[..., width:], 2)
        env = env.reshape(mw, groups, GROUP, chi_in)
        for g in range(groups):
            lhs[g * part : (g + 1) * part, :] = env[:, g].reshape(part, chi_in).astype(jnp.bfloat16)

        def state(k, _):
            @pl.when(i == 0)
            def _():
                for copy in wave_copies(k):
                    copy.wait()

                @pl.when(k == 0)
                def _():
                    here_copy.wait()

            here = here_ref[k, pl.ds(pl.multiple_of(i * rows, rows), rows)]
            at = pl.multiple_of((k * blocks + i) * rows * phys, rows * phys)
            turned[:, pl.ds(at, rows * phys)] = here.reshape(rows * phys, chi).T
            for t in range(phys):
                inner = product(lhs[...], wave_ref[k, t], ((1,), (0,))).astype(jnp.bfloat16)
                low[:, t * part : (t + 1) * part, :] = inner.reshape(groups, part, chi)
            for g in range(groups):
                through = product(table, low[g], ((1,), (0,))).astype(jnp.bfloat16)
                size = GROUP * phys
                at = pl.multiple_of(i * rows * phys + g * size, size)
                through_ref[:, k, pl.ds(at, size), :] = through.reshape(mw, size, chi)
            return 0

        lax.fori_loop(0, num_states, state, 0)
        for copy in through_copies(i):
            copy.start()
        return 0

    lax.fori_loop(0, blocks, block, 0)

    depth = rows_all * phys

    def out_copies(v, slot):
        return [
            pltpu.make_async_copy(
                stage.at[slot, pl.ds(index * (chi // parts), chi // parts)],
                out.at[v],
                out_sems.at[slot, index],
            )
            for index, out in enumerate(outs)
        ]

    def bond(v, _):
        slot = v % 2
        right = through_ref[v].reshape(num_states * depth, chi)
        share = (product(turned[...], right, ((1,), (0,))) * scaling).astype(jnp.bfloat16)
        if parts == 2:
            share = own_first(swap, share[: chi // 2], share[chi // 2 :], 0)

        @pl.when(v >= 2)
        def _():
            for copy in out_copies(v - 2, slot):
                copy.wait()

        stage[slot] = share
        for copy in out_copies(v, slot):
            copy.start()
        return 0

    lax.fori_loop(0, mw, bond, 0)
    for v in range(max(mw - 2, 0), mw):
        for copy in out_copies(v, v % 2):
            copy.wait()
    for i in range(blocks):
        for copy in through_copies(i):
            copy.wait()
    token_ref[...] = jnp.zeros_like(token_ref)


def sweep(bonds, env, here, waves, places, counts, scaling):
    mw, rows_all, chi_in = env.shape
    phys, _, chi = waves[0][0].shape[1:]
    num_states = here.shape[1]
    rows = min(64, rows_all)
    parts = len(waves[0])
    padded = -(-mw * phys * GROUP // 128) * 128
    bf16 = jnp.bfloat16
    share = jax.ShapeDtypeStruct((mw, chi // parts, chi), bf16)
    out = pl.pallas_call(
        functools.partial(sweep_kernel, parts, len(waves), len(counts), scaling),
        in_specs=[SCALARS, WHOLE] + [ANY] * (2 + parts * len(waves)),
        out_specs=[ANY] * len(counts) + [WHOLE] + [ANY] * parts,
        scratch_shapes=[
            pltpu.VMEM(env.shape, bf16),
            pltpu.VMEM(here.shape[1:], bf16),
            pltpu.VMEM((num_states, phys, chi_in, chi), bf16),
            pltpu.VMEM((mw * rows, chi_in), bf16),
            pltpu.VMEM((rows // GROUP, padded, chi), bf16),
            pltpu.VMEM((chi, num_states * rows_all * phys), bf16),
            pltpu.VMEM((2, chi, chi), bf16),
            pltpu.VMEM((mw, num_states, rows_all * phys, chi), bf16),
            pltpu.SemaphoreType.DMA((rows_all // rows,)),
            pltpu.SemaphoreType.DMA((num_states, parts)),
            pltpu.SemaphoreType.DMA,
            pltpu.SemaphoreType.DMA((2, parts)),
            pltpu.SemaphoreType.DMA((rows_all // rows, len(counts))),
        ],
        out_shape=[
            jax.ShapeDtypeStruct((count, num_states, rows_all * phys, chi), bf16)
            for count in counts
        ]
        + [TOKEN]
        + [share] * parts,
        compiler_params=pltpu.CompilerParams(vmem_limit_bytes=SWEEP_MIB * MIB),
        cost_estimate=pl.CostEstimate(
            flops=0,
            bytes_accessed=0,
            transcendentals=0,
        ),
        name="sweep",
    )(places, bonds, env, here, *[wave for turn in waves for wave in turn])
    pieces = len(counts)
    return out[:pieces], out[pieces], out[pieces + 1 :]


def applied_kernel(parts, pieces, begun, close, places, through_in, *refs):
    rights, refs = refs[: parts * pieces], refs[parts * pieces :]
    if begun:
        held, refs = refs[0], refs[1:]
    out, token_ref, turned, refs = refs[0], refs[1], refs[2], refs[3:]
    last = out.dtype == jnp.bfloat16
    count, num_states, rows, chi = through_in.shape
    if last:
        results, out_sems, refs = refs[0], refs[1], refs[2:]
    if close:
        through_ref = through_in
    else:
        through_ref, through_sems = refs

    def through_copies(k):
        return [
            pltpu.make_async_copy(through_in.at[v, k], through_ref.at[v, k], through_sems.at[v, k])
            for v in range(count)
        ]

    def out_copy(k, slot):
        return pltpu.make_async_copy(results.at[slot], out.at[k], out_sems.at[slot])

    if not close:
        for k in range(num_states):
            for copy in through_copies(k):
                copy.start()
    def turn(v):
        for piece in range(pieces):
            blocks = rights[piece * parts : (piece + 1) * parts]
            n = v - sum(rights[before * parts].shape[0] for before in range(piece))
            if 0 <= n < blocks[0].shape[0]:
                right = jnp.concatenate([block[n] for block in blocks], axis=0)
                turned[v * chi : (v + 1) * chi, :] = right.T

    def state(k, _):
        if not close:
            for copy in through_copies(k):
                copy.wait()
        if isinstance(k, int) and k == 0:
            total = None
            for v in range(0, count, 2):
                most = min(v + 2, count)
                for n in range(v, most):
                    turn(n)
                left = jnp.concatenate([through_ref[n, k] for n in range(v, most)], axis=1)
                term = product(left, turned[v * chi : most * chi, :], ((1,), (0,)))
                total = term if total is None else total + term
        else:
            left = jnp.concatenate([through_ref[v, k] for v in range(count)], axis=1)
            total = product(left, turned[...], ((1,), (0,)))
        if begun:
            total = total + held[k]
        if not last:
            out[k] = total
            return 0
        columns = total.shape[1]
        phys = results.shape[2]
        total = total.astype(jnp.bfloat16)
        if parts == 2:
            swap = places[0] != 0
            total = own_first(swap, total[:, : columns // 2], total[:, columns // 2 :], 1)
        slot = k % 2

        if k >= 2:
            out_copy(k - 2, slot).wait()
        results[slot] = total.reshape(rows // phys, phys, columns)
        out_copy(k, slot).start()
        return 0

    state(0, 0)
    if last:
        for k in range(1, num_states):
            state(k, 0)
    else:
        lax.fori_loop(1, num_states, state, 0)
    if last:
        for k in range(max(num_states - 2, 0), num_states):
            out_copy(k, k % 2).wait()
    token_ref[...] = jnp.zeros_like(token_ref)


def applied_part(through, rights, held, places, phys, last):
    count, num_states, rows, chi = through.shape
    width = rights[0][0].shape[1]
    parts = len(rights[0])
    begun = held is not None
    close = count <= 4
    columns = width * parts
    scratch = [pltpu.VMEM((count * chi, columns), jnp.bfloat16)]
    if last:
        shape = (num_states, rows // phys, phys, columns)
        out_shape, out_spec = jax.ShapeDtypeStruct(shape, jnp.bfloat16), ANY
        scratch += [pltpu.VMEM((2,) + shape[1:], jnp.bfloat16), pltpu.SemaphoreType.DMA((2,))]
    else:
        out_shape, out_spec = pltpu.VMEM((num_states, rows, columns), jnp.float32), WHOLE
    if not close:
        scratch += [
            pltpu.VMEM(through.shape, jnp.bfloat16),
            pltpu.SemaphoreType.DMA((count, num_states)),
        ]
    operands = [near(through) if close else far(through)]
    operands += [near(block) for blocks in rights for block in blocks] + ([near(held)] if begun else [])
    return pl.pallas_call(
        functools.partial(applied_kernel, parts, len(rights), begun, close),
        in_specs=[SCALARS, WHOLE if close else ANY] + [WHOLE] * (len(operands) - 1),
        out_specs=[out_spec, WHOLE],
        out_shape=[out_shape, TOKEN],
        scratch_shapes=scratch,
        compiler_params=pltpu.CompilerParams(vmem_limit_bytes=(16 if close else 34) * MIB),
        cost_estimate=pl.CostEstimate(
            flops=0,
            bytes_accessed=0,
            transcendentals=0,
        ),
        name="applied_part",
    )(places, *operands)


def cuts(size):
    first = (size - 1) * 6 // 13
    return [[count] for count in (first, size - 1 - first, 1) if count > 0]


def on_device(left_env, right_env, states, mpo):
    num_states, rows, phys, chi = states.shape[1:]
    mw = mpo.shape[0]
    bonds = lax.axis_size("bond")
    paired = bonds == 2
    me = lax.axis_index("bond").astype(jnp.int32)
    places = jnp.stack([me, 1 - me]) if paired else jnp.stack([me, me]) * 0
    scaling = 1.0 / math.sqrt(num_states * chi)
    left = left_env[0].transpose(1, 0, 2)
    right = right_env[0].transpose(1, 0, 2)

    stages = cuts(mw)
    pieces, first = [], 0
    for stage in stages:
        pieces.append([])
        for count in stage:
            piece = passed_along(right[first : first + count], "seg", -1)
            pieces[-1].append(piece)
            first += count

    half = max(num_states // 2, 1)
    waves = []
    for start in range(0, num_states, half):
        wave = states[0, start : start + half].transpose(0, 2, 1, 3)
        if paired:
            waves.append([wave, swapped(wave, "bond")])
        else:
            waves.append([lax.all_gather(wave, "bond", axis=2, tiled=True)])
    bond_table = mpo.transpose(3, 1, 2, 0).reshape(mw * phys, phys * mw)
    counts = [sum(stage) for stage in stages]
    throughs, token, shares = sweep(bond_table, left, states, waves, places, counts, scaling)
    if paired:
        arrived = swapped(shares[1], "bond")
        new_env = shares[0].astype(jnp.float32) + arrived.astype(jnp.float32)
        new_env = new_env.astype(jnp.bfloat16)
    else:
        new_env = lax.psum_scatter(shares[0], "bond", scatter_dimension=1, tiled=True)

    held = None
    for index, (through, stage) in enumerate(zip(throughs, pieces)):
        rights = []
        for piece in stage:
            if paired:
                piece = after(piece, token)
                rights.append([piece, swapped(piece, "bond")])
            else:
                rights.append([lax.all_gather(piece, "bond", axis=1, tiled=True)])
        last = index == len(pieces) - 1
        held, token = applied_part(through, rights, held, places, phys, last)
    return (held[None], new_env.transpose(1, 0, 2)[None])


def solution(mesh):
    in_specs = (
        P("seg", "bond", None, None),
        P("seg", "bond", None, None),
        P("seg", None, "bond", None, None),
        P(),
    )
    out_specs = (P("seg", None, "bond", None, None), P("seg", "bond", None, None))
    return jax.shard_map(
        on_device, mesh=mesh, in_specs=in_specs, out_specs=out_specs, check_vma=False
    )
```

```python
import functools
import math

import jax
import jax.numpy as jnp
from jax import lax
from jax.experimental import pallas as pl
from jax.experimental.pallas import tpu as pltpu
from jax.sharding import PartitionSpec as P

GROUP = 8
MIB = 1 << 20
SWEEP_MIB = 54
ANY = pl.BlockSpec(memory_space=pl.ANY)
TOKEN = pltpu.VMEM((8, 128), jnp.float32)
WHOLE = pl.BlockSpec(memory_space=pltpu.VMEM)


def passed_along(array, axis, by):
    size = lax.axis_size(axis)
    pairs = [(i, i + by) for i in range(size) if 0 <= i + by < size]
    return lax.ppermute(array, axis, pairs)


def swapped(array, axis):
    return lax.ppermute(array, axis, [(0, 1), (1, 0)])


def product(left, right, contract):
    return lax.dot_general(left, right, (contract, ((), ())), preferred_element_type=jnp.float32)


def near(array):
    return pltpu.with_memory_space_constraint(array, pltpu.VMEM)


def far(array):
    return pltpu.with_memory_space_constraint(array, pltpu.HBM)


def after(array, token):
    return pl.pallas_call(
        lambda *refs: None,
        in_specs=[ANY, WHOLE],
        out_specs=ANY,
        out_shape=jax.ShapeDtypeStruct(array.shape, array.dtype),
        input_output_aliases={0: 0},
        compiler_params=pltpu.CompilerParams(vmem_limit_bytes=MIB),
        name="after",
    )(array, near(token))


def cut(array, at, count):
    def kernel(in_ref, out_ref, sems):
        copies = [
            pltpu.make_async_copy(in_ref.at[at + n], out_ref.at[n], sems.at[n])
            for n in range(count)
        ]
        for copy in copies:
            copy.start()
        for copy in copies:
            copy.wait()

    return pl.pallas_call(
        kernel,
        in_specs=[ANY],
        out_specs=ANY,
        out_shape=jax.ShapeDtypeStruct((count,) + array.shape[1:], array.dtype),
        scratch_shapes=[pltpu.SemaphoreType.DMA((count,))],
        compiler_params=pltpu.CompilerParams(vmem_limit_bytes=MIB),
        name="cut",
    )(far(array))


def block_diagonal(bonds, mw, phys):
    size = mw * phys
    full = size * GROUP
    row = lax.broadcasted_iota(jnp.int32, (full, size), 0)
    which = lax.broadcasted_iota(jnp.int32, (full, size), 1)
    pick_row = (row // (GROUP * phys) * phys + row % phys == which).astype(jnp.bfloat16)
    column = lax.broadcasted_iota(jnp.int32, (size, full), 1)
    which = lax.broadcasted_iota(jnp.int32, (size, full), 0)
    pick_column = (column // GROUP == which).astype(jnp.bfloat16)
    spread = product(pick_row, bonds, ((1,), (0,))).astype(jnp.bfloat16)
    spread = product(spread, pick_column, ((1,), (0,)))
    row = lax.broadcasted_iota(jnp.int32, (full, full), 0)
    column = lax.broadcasted_iota(jnp.int32, (full, full), 1)
    same = row % (GROUP * phys) // phys == column % GROUP
    return jnp.where(same, spread, 0.0).astype(jnp.bfloat16)


def own_first(swap, first, second, axis):
    return jnp.concatenate(
        [jnp.where(swap, second, first), jnp.where(swap, first, second)], axis=axis
    )


def sweep_kernel(parts, turns, pieces, scaling, bonds_ref, env_hbm, here_hbm, *refs):
    waves_hbm, refs = refs[: parts * turns], refs[parts * turns :]
    throughs_hbm, refs = refs[:pieces], refs[pieces:]
    token_ref, refs = refs[0], refs[1:]
    outs, refs = refs[:parts], refs[parts:]
    env_ref, here_ref, wave_ref, lhs, low, turned, stage, through_ref = refs[:8]
    env_sems, wave_sems, here_sem, out_sems, through_sems = refs[8:]
    mw, rows_all, chi_in = env_ref.shape
    num_states, phys, _, chi = wave_ref.shape
    width = chi_in // parts
    part = mw * GROUP
    groups = lhs.shape[0] // part
    rows = groups * GROUP
    blocks = rows_all // rows

    def env_copy(i):
        here = pl.ds(pl.multiple_of(i * rows, rows), rows)
        return pltpu.make_async_copy(env_hbm.at[:, here], env_ref.at[:, here], env_sems.at[i])

    def wave_starts(k):
        turn, inside = divmod(k, waves_hbm[0].shape[0])
        return [
            pltpu.make_async_copy(
                waves_hbm[turn * parts + index].at[inside],
                wave_ref.at[k, :, pl.ds(index * width, width)],
                wave_sems.at[k, index],
            )
            for index in range(parts)
        ]

    def wave_copies(k):
        return [
            pltpu.make_async_copy(
                waves_hbm[index].at[0],
                wave_ref.at[k, :, pl.ds(index * width, width)],
                wave_sems.at[k, index],
            )
            for index in range(parts)
        ]

    def through_copies(i):
        here = pl.ds(pl.multiple_of(i * rows * phys, rows * phys), rows * phys)
        found, first = [], 0
        for index, out in enumerate(throughs_hbm):
            count = out.shape[0]
            found.append(
                pltpu.make_async_copy(
                    through_ref.at[pl.ds(first, count), :, here],
                    out.at[:, :, here],
                    through_sems.at[i, index],
                )
            )
            first += count
        return found

    here_copy = pltpu.make_async_copy(here_hbm.at[0], here_ref, here_sem)
    for n in range(max(blocks, num_states)):
        if n < blocks:
            env_copy(n).start()
        if n < num_states:
            for copy in wave_starts(n):
                copy.start()
    here_copy.start()

    table = block_diagonal(bonds_ref[...], mw, phys)
    depth = table.shape[0]
    padded = low.shape[1]
    table = jnp.concatenate([table, jnp.zeros((depth, padded - depth), table.dtype)], axis=1)
    low[:, depth:, :] = jnp.zeros((groups, padded - depth, chi), low.dtype)
    swap = lax.axis_index("bond") != 0

    def block(i, _):
        env_copy(i).wait()
        env = env_ref[:, pl.ds(pl.multiple_of(i * rows, rows), rows), :].astype(jnp.float32)
        if parts == 2:
            env = own_first(swap, env[..., :width], env[..., width:], 2)
        env = env.reshape(mw, groups, GROUP, chi_in)
        for g in range(groups):
            lhs[g * part : (g + 1) * part, :] = env[:, g].reshape(part, chi_in).astype(jnp.bfloat16)

        def state(k, _):
            @pl.when(i == 0)
            def _():
                for copy in wave_copies(k):
                    copy.wait()

                @pl.when(k == 0)
                def _():
                    here_copy.wait()

            here = here_ref[k, pl.ds(pl.multiple_of(i * rows, rows), rows)]
            at = pl.multiple_of((k * blocks + i) * rows * phys, rows * phys)
            turned[:, pl.ds(at, rows * phys)] = here.reshape(rows * phys, chi).T
            for t in range(phys):
                inner = product(lhs[...], wave_ref[k, t], ((1,), (0,))).astype(jnp.bfloat16)
                low[:, t * part : (t + 1) * part, :] = inner.reshape(groups, part, chi)
            for g in range(groups):
                through = product(table, low[g], ((1,), (0,))).astype(jnp.bfloat16)
                size = GROUP * phys
                at = pl.multiple_of(i * rows * phys + g * size, size)
                through_ref[:, k, pl.ds(at, size), :] = through.reshape(mw, size, chi)
            return 0

        lax.fori_loop(0, num_states, state, 0)
        for copy in through_copies(i):
            copy.start()
        return 0

    lax.fori_loop(0, blocks, block, 0)

    depth = rows_all * phys

    def out_copies(v, slot):
        return [
            pltpu.make_async_copy(
                stage.at[slot, pl.ds(index * (chi // parts), chi // parts)],
                out.at[v],
                out_sems.at[slot, index],
            )
            for index, out in enumerate(outs)
        ]

    def bond(v, _):
        slot = v % 2
        right = through_ref[v].reshape(num_states * depth, chi)
        share = (product(turned[...], right, ((1,), (0,))) * scaling).astype(jnp.bfloat16)
        if parts == 2:
            share = own_first(swap, share[: chi // 2], share[chi // 2 :], 0)

        @pl.when(v >= 2)
        def _():
            for copy in out_copies(v - 2, slot):
                copy.wait()

        stage[slot] = share
        for copy in out_copies(v, slot):
            copy.start()
        return 0

    lax.fori_loop(0, mw, bond, 0)
    for v in range(max(mw - 2, 0), mw):
        for copy in out_copies(v, v % 2):
            copy.wait()
    for i in range(blocks):
        for copy in through_copies(i):
            copy.wait()
    token_ref[...] = jnp.zeros_like(token_ref)


def sweep(bonds, env, here, waves, counts, scaling):
    mw, rows_all, chi_in = env.shape
    phys, _, chi = waves[0][0].shape[1:]
    num_states = here.shape[1]
    rows = min(64, rows_all)
    parts = len(waves[0])
    padded = -(-mw * phys * GROUP // 128) * 128
    bf16 = jnp.bfloat16
    share = jax.ShapeDtypeStruct((mw, chi // parts, chi), bf16)
    out = pl.pallas_call(
        functools.partial(sweep_kernel, parts, len(waves), len(counts), scaling),
        in_specs=[WHOLE] + [ANY] * (2 + parts * len(waves)),
        out_specs=[ANY] * len(counts) + [WHOLE] + [ANY] * parts,
        scratch_shapes=[
            pltpu.VMEM(env.shape, bf16),
            pltpu.VMEM(here.shape[1:], bf16),
            pltpu.VMEM((num_states, phys, chi_in, chi), bf16),
            pltpu.VMEM((mw * rows, chi_in), bf16),
            pltpu.VMEM((rows // GROUP, padded, chi), bf16),
            pltpu.VMEM((chi, num_states * rows_all * phys), bf16),
            pltpu.VMEM((2, chi, chi), bf16),
            pltpu.VMEM((mw, num_states, rows_all * phys, chi), bf16),
            pltpu.SemaphoreType.DMA((rows_all // rows,)),
            pltpu.SemaphoreType.DMA((num_states, parts)),
            pltpu.SemaphoreType.DMA,
            pltpu.SemaphoreType.DMA((2, parts)),
            pltpu.SemaphoreType.DMA((rows_all // rows, len(counts))),
        ],
        out_shape=[
            jax.ShapeDtypeStruct((count, num_states, rows_all * phys, chi), bf16)
            for count in counts
        ]
        + [TOKEN]
        + [share] * parts,
        compiler_params=pltpu.CompilerParams(vmem_limit_bytes=SWEEP_MIB * MIB),
        cost_estimate=pl.CostEstimate(
            flops=0,
            bytes_accessed=0,
            transcendentals=0,
        ),
        name="sweep",
    )(bonds, env, here, *[wave for turn in waves for wave in turn])
    pieces = len(counts)
    return out[:pieces], out[pieces], out[pieces + 1 :]


def applied_kernel(parts, pieces, begun, close, through_in, *refs):
    rights, refs = refs[: parts * pieces], refs[parts * pieces :]
    if begun:
        held, refs = refs[0], refs[1:]
    out, token_ref, turned, refs = refs[0], refs[1], refs[2], refs[3:]
    last = out.dtype == jnp.bfloat16
    count, num_states, rows, chi = through_in.shape
    if last:
        results, out_sems, refs = refs[0], refs[1], refs[2:]
    if close:
        through_ref = through_in
    else:
        through_ref, through_sems = refs

    def through_copies(k):
        return [
            pltpu.make_async_copy(through_in.at[v, k], through_ref.at[v, k], through_sems.at[v, k])
            for v in range(count)
        ]

    def out_copy(k, slot):
        return pltpu.make_async_copy(results.at[slot], out.at[k], out_sems.at[slot])

    if not close:
        for k in range(num_states):
            for copy in through_copies(k):
                copy.start()
    def turn(v):
        for piece in range(pieces):
            blocks = rights[piece * parts : (piece + 1) * parts]
            n = v - sum(rights[before * parts].shape[0] for before in range(piece))
            if 0 <= n < blocks[0].shape[0]:
                right = jnp.concatenate([block[n] for block in blocks], axis=0)
                turned[v * chi : (v + 1) * chi, :] = right.T

    def state(k, _):
        if not close:
            for copy in through_copies(k):
                copy.wait()
        if isinstance(k, int) and k == 0:
            total = None
            for v in range(0, count, 2):
                most = min(v + 2, count)
                for n in range(v, most):
                    turn(n)
                left = jnp.concatenate([through_ref[n, k] for n in range(v, most)], axis=1)
                term = product(left, turned[v * chi : most * chi, :], ((1,), (0,)))
                total = term if total is None else total + term
        else:
            left = jnp.concatenate([through_ref[v, k] for v in range(count)], axis=1)
            total = product(left, turned[...], ((1,), (0,)))
        if begun:
            total = total + held[k]
        if not last:
            out[k] = total
            return 0
        columns = total.shape[1]
        phys = results.shape[2]
        total = total.astype(jnp.bfloat16)
        if parts == 2:
            swap = lax.axis_index("bond") != 0
            total = own_first(swap, total[:, : columns // 2], total[:, columns // 2 :], 1)
        slot = k % 2

        if k >= 2:
            out_copy(k - 2, slot).wait()
        results[slot] = total.reshape(rows // phys, phys, columns)
        out_copy(k, slot).start()
        return 0

    state(0, 0)
    if last:
        for k in range(1, num_states):
            state(k, 0)
    else:
        lax.fori_loop(1, num_states, state, 0)
    if last:
        for k in range(max(num_states - 2, 0), num_states):
            out_copy(k, k % 2).wait()
    token_ref[...] = jnp.zeros_like(token_ref)


def applied_part(through, rights, held, phys, last):
    count, num_states, rows, chi = through.shape
    width = rights[0][0].shape[1]
    parts = len(rights[0])
    begun = held is not None
    close = count <= 4
    columns = width * parts
    scratch = [pltpu.VMEM((count * chi, columns), jnp.bfloat16)]
    if last:
        shape = (num_states, rows // phys, phys, columns)
        out_shape, out_spec = jax.ShapeDtypeStruct(shape, jnp.bfloat16), ANY
        scratch += [pltpu.VMEM((2,) + shape[1:], jnp.bfloat16), pltpu.SemaphoreType.DMA((2,))]
    else:
        out_shape, out_spec = pltpu.VMEM((num_states, rows, columns), jnp.float32), WHOLE
    if not close:
        scratch += [
            pltpu.VMEM(through.shape, jnp.bfloat16),
            pltpu.SemaphoreType.DMA((count, num_states)),
        ]
    operands = [near(through) if close else far(through)]
    operands += [near(block) for blocks in rights for block in blocks] + ([near(held)] if begun else [])
    return pl.pallas_call(
        functools.partial(applied_kernel, parts, len(rights), begun, close),
        in_specs=[WHOLE if close else ANY] + [WHOLE] * (len(operands) - 1),
        out_specs=[out_spec, WHOLE],
        out_shape=[out_shape, TOKEN],
        scratch_shapes=scratch,
        compiler_params=pltpu.CompilerParams(vmem_limit_bytes=(16 if close else 34) * MIB),
        cost_estimate=pl.CostEstimate(
            flops=0,
            bytes_accessed=0,
            transcendentals=0,
        ),
        name="applied_part",
    )(*operands)


def cuts(size):
    first = (size - 1) * 6 // 13
    return [[count] for count in (first, size - 1 - first, 1) if count > 0]


def on_device(left_env, right_env, states, mpo):
    num_states, rows, phys, chi = states.shape[1:]
    mw = mpo.shape[0]
    bonds = lax.axis_size("bond")
    paired = bonds == 2
    scaling = 1.0 / math.sqrt(num_states * chi)
    left = left_env[0].transpose(1, 0, 2)
    right = right_env[0].transpose(1, 0, 2)

    stages = cuts(mw)
    pieces, first = [], 0
    for stage in stages:
        pieces.append([])
        for count in stage:
            piece = passed_along(cut(right, first, count), "seg", -1)
            pieces[-1].append(piece)
            first += count

    half = max(num_states // 2, 1)
    waves = []
    for start in range(0, num_states, half):
        wave = states[0, start : start + half].transpose(0, 2, 1, 3)
        if paired:
            waves.append([wave, swapped(wave, "bond")])
        else:
            waves.append([lax.all_gather(wave, "bond", axis=2, tiled=True)])
    bond_table = mpo.transpose(3, 1, 2, 0).reshape(mw * phys, phys * mw)
    counts = [sum(stage) for stage in stages]
    throughs, token, shares = sweep(bond_table, left, states, waves, counts, scaling)
    if paired:
        arrived = swapped(shares[1], "bond")
        new_env = shares[0].astype(jnp.float32) + arrived.astype(jnp.float32)
        new_env = new_env.astype(jnp.bfloat16)
    else:
        new_env = lax.psum_scatter(shares[0], "bond", scatter_dimension=1, tiled=True)

    held = None
    for index, (through, stage) in enumerate(zip(throughs, pieces)):
        rights = []
        for piece in stage:
            if paired:
                piece = after(piece, token)
                rights.append([piece, swapped(piece, "bond")])
            else:
                rights.append([lax.all_gather(piece, "bond", axis=1, tiled=True)])
        last = index == len(pieces) - 1
        held, token = applied_part(through, rights, held, phys, last)
    return (held[None], new_env.transpose(1, 0, 2)[None])


def solution(mesh):
    in_specs = (
        P("seg", "bond", None, None),
        P("seg", "bond", None, None),
        P("seg", None, "bond", None, None),
        P(),
    )
    out_specs = (P("seg", None, "bond", None, None), P("seg", "bond", None, None))
    return jax.shard_map(
        on_device, mesh=mesh, in_specs=in_specs, out_specs=out_specs, check_vma=False
    )
```

```python
import functools
import math

import jax
import jax.numpy as jnp
from jax import lax
from jax.experimental import pallas as pl
from jax.experimental.pallas import tpu as pltpu
from jax.sharding import PartitionSpec as P

GROUP = 8
MIB = 1 << 20
SWEEP_MIB = 54
ANY = pl.BlockSpec(memory_space=pl.ANY)
TOKEN = pltpu.VMEM((8, 128), jnp.float32)
WHOLE = pl.BlockSpec(memory_space=pltpu.VMEM)


def passed_along(array, axis, by):
    size = lax.axis_size(axis)
    pairs = [(i, i + by) for i in range(size) if 0 <= i + by < size]
    return lax.ppermute(array, axis, pairs)


def swapped(array, axis):
    return lax.ppermute(array, axis, [(0, 1), (1, 0)])


def product(left, right, contract):
    return lax.dot_general(left, right, (contract, ((), ())), preferred_element_type=jnp.float32)


def near(array):
    return pltpu.with_memory_space_constraint(array, pltpu.VMEM)


def far(array):
    return pltpu.with_memory_space_constraint(array, pltpu.HBM)


def after(array, token):
    return pl.pallas_call(
        lambda *refs: None,
        in_specs=[ANY, WHOLE],
        out_specs=ANY,
        out_shape=jax.ShapeDtypeStruct(array.shape, array.dtype),
        input_output_aliases={0: 0},
        compiler_params=pltpu.CompilerParams(vmem_limit_bytes=MIB),
        name="after",
    )(array, near(token))


def cut(array, at, count):
    def kernel(in_ref, out_ref, sems):
        copies = [
            pltpu.make_async_copy(in_ref.at[at + n], out_ref.at[n], sems.at[n])
            for n in range(count)
        ]
        for copy in copies:
            copy.start()
        for copy in copies:
            copy.wait()

    return pl.pallas_call(
        kernel,
        in_specs=[ANY],
        out_specs=WHOLE,
        out_shape=pltpu.VMEM((count,) + array.shape[1:], array.dtype),
        scratch_shapes=[pltpu.SemaphoreType.DMA((count,))],
        compiler_params=pltpu.CompilerParams(vmem_limit_bytes=8 * MIB),
        name="cut",
    )(far(array))


def block_diagonal(bonds, mw, phys):
    size = mw * phys
    full = size * GROUP
    row = lax.broadcasted_iota(jnp.int32, (full, size), 0)
    which = lax.broadcasted_iota(jnp.int32, (full, size), 1)
    pick_row = (row // (GROUP * phys) * phys + row % phys == which).astype(jnp.bfloat16)
    column = lax.broadcasted_iota(jnp.int32, (size, full), 1)
    which = lax.broadcasted_iota(jnp.int32, (size, full), 0)
    pick_column = (column // GROUP == which).astype(jnp.bfloat16)
    spread = product(pick_row, bonds, ((1,), (0,))).astype(jnp.bfloat16)
    spread = product(spread, pick_column, ((1,), (0,)))
    row = lax.broadcasted_iota(jnp.int32, (full, full), 0)
    column = lax.broadcasted_iota(jnp.int32, (full, full), 1)
    same = row % (GROUP * phys) // phys == column % GROUP
    return jnp.where(same, spread, 0.0).astype(jnp.bfloat16)


def own_first(swap, first, second, axis):
    return jnp.concatenate(
        [jnp.where(swap, second, first), jnp.where(swap, first, second)], axis=axis
    )


def sweep_kernel(parts, turns, pieces, scaling, bonds_ref, env_hbm, here_hbm, *refs):
    waves_hbm, refs = refs[: parts * turns], refs[parts * turns :]
    throughs_hbm, refs = refs[:pieces], refs[pieces:]
    token_ref, refs = refs[0], refs[1:]
    outs, refs = refs[:parts], refs[parts:]
    env_ref, here_ref, wave_ref, lhs, low, turned, stage, through_ref = refs[:8]
    env_sems, wave_sems, here_sem, out_sems, through_sems = refs[8:]
    mw, rows_all, chi_in = env_ref.shape
    num_states, phys, _, chi = wave_ref.shape
    width = chi_in // parts
    part = mw * GROUP
    groups = lhs.shape[0] // part
    rows = groups * GROUP
    blocks = rows_all // rows

    def env_copy(i):
        here = pl.ds(pl.multiple_of(i * rows, rows), rows)
        return pltpu.make_async_copy(env_hbm.at[:, here], env_ref.at[:, here], env_sems.at[i])

    def wave_starts(k):
        turn, inside = divmod(k, waves_hbm[0].shape[0])
        return [
            pltpu.make_async_copy(
                waves_hbm[turn * parts + index].at[inside],
                wave_ref.at[k, :, pl.ds(index * width, width)],
                wave_sems.at[k, index],
            )
            for index in range(parts)
        ]

    def wave_copies(k):
        return [
            pltpu.make_async_copy(
                waves_hbm[index].at[0],
                wave_ref.at[k, :, pl.ds(index * width, width)],
                wave_sems.at[k, index],
            )
            for index in range(parts)
        ]

    def through_copies(i):
        here = pl.ds(pl.multiple_of(i * rows * phys, rows * phys), rows * phys)
        found, first = [], 0
        for index, out in enumerate(throughs_hbm):
            count = out.shape[0]
            found.append(
                pltpu.make_async_copy(
                    through_ref.at[pl.ds(first, count), :, here],
                    out.at[:, :, here],
                    through_sems.at[i, index],
                )
            )
            first += count
        return found

    here_copy = pltpu.make_async_copy(here_hbm.at[0], here_ref, here_sem)
    for n in range(max(blocks, num_states)):
        if n < blocks:
            env_copy(n).start()
        if n < num_states:
            for copy in wave_starts(n):
                copy.start()
    here_copy.start()

    table = block_diagonal(bonds_ref[...], mw, phys)
    depth = table.shape[0]
    padded = low.shape[1]
    table = jnp.concatenate([table, jnp.zeros((depth, padded - depth), table.dtype)], axis=1)
    low[:, depth:, :] = jnp.zeros((groups, padded - depth, chi), low.dtype)
    swap = lax.axis_index("bond") != 0

    def block(i, _):
        env_copy(i).wait()
        env = env_ref[:, pl.ds(pl.multiple_of(i * rows, rows), rows), :].astype(jnp.float32)
        if parts == 2:
            env = own_first(swap, env[..., :width], env[..., width:], 2)
        env = env.reshape(mw, groups, GROUP, chi_in)
        for g in range(groups):
            lhs[g * part : (g + 1) * part, :] = env[:, g].reshape(part, chi_in).astype(jnp.bfloat16)

        def state(k, _):
            @pl.when(i == 0)
            def _():
                for copy in wave_copies(k):
                    copy.wait()

                @pl.when(k == 0)
                def _():
                    here_copy.wait()

            here = here_ref[k, pl.ds(pl.multiple_of(i * rows, rows), rows)]
            at = pl.multiple_of((k * blocks + i) * rows * phys, rows * phys)
            turned[:, pl.ds(at, rows * phys)] = here.reshape(rows * phys, chi).T
            for t in range(phys):
                inner = product(lhs[...], wave_ref[k, t], ((1,), (0,))).astype(jnp.bfloat16)
                low[:, t * part : (t + 1) * part, :] = inner.reshape(groups, part, chi)
            for g in range(groups):
                through = product(table, low[g], ((1,), (0,))).astype(jnp.bfloat16)
                size = GROUP * phys
                at = pl.multiple_of(i * rows * phys + g * size, size)
                through_ref[:, k, pl.ds(at, size), :] = through.reshape(mw, size, chi)
            return 0

        lax.fori_loop(0, num_states, state, 0)
        for copy in through_copies(i):
            copy.start()
        return 0

    lax.fori_loop(0, blocks, block, 0)

    depth = rows_all * phys

    def out_copies(v, slot):
        return [
            pltpu.make_async_copy(
                stage.at[slot, pl.ds(index * (chi // parts), chi // parts)],
                out.at[v],
                out_sems.at[slot, index],
            )
            for index, out in enumerate(outs)
        ]

    def bond(v, _):
        slot = v % 2
        right = through_ref[v].reshape(num_states * depth, chi)
        share = (product(turned[...], right, ((1,), (0,))) * scaling).astype(jnp.bfloat16)
        if parts == 2:
            share = own_first(swap, share[: chi // 2], share[chi // 2 :], 0)

        @pl.when(v >= 2)
        def _():
            for copy in out_copies(v - 2, slot):
                copy.wait()

        stage[slot] = share
        for copy in out_copies(v, slot):
            copy.start()
        return 0

    lax.fori_loop(0, mw, bond, 0)
    for v in range(max(mw - 2, 0), mw):
        for copy in out_copies(v, v % 2):
            copy.wait()
    for i in range(blocks):
        for copy in through_copies(i):
            copy.wait()
    token_ref[...] = jnp.zeros_like(token_ref)


def sweep(bonds, env, here, waves, counts, scaling):
    mw, rows_all, chi_in = env.shape
    phys, _, chi = waves[0][0].shape[1:]
    num_states = here.shape[1]
    rows = min(64, rows_all)
    parts = len(waves[0])
    padded = -(-mw * phys * GROUP // 128) * 128
    bf16 = jnp.bfloat16
    share = jax.ShapeDtypeStruct((mw, chi // parts, chi), bf16)
    out = pl.pallas_call(
        functools.partial(sweep_kernel, parts, len(waves), len(counts), scaling),
        in_specs=[WHOLE] + [ANY] * (2 + parts * len(waves)),
        out_specs=[ANY] * len(counts) + [WHOLE] + [ANY] * parts,
        scratch_shapes=[
            pltpu.VMEM(env.shape, bf16),
            pltpu.VMEM(here.shape[1:], bf16),
            pltpu.VMEM((num_states, phys, chi_in, chi), bf16),
            pltpu.VMEM((mw * rows, chi_in), bf16),
            pltpu.VMEM((rows // GROUP, padded, chi), bf16),
            pltpu.VMEM((chi, num_states * rows_all * phys), bf16),
            pltpu.VMEM((2, chi, chi), bf16),
            pltpu.VMEM((mw, num_states, rows_all * phys, chi), bf16),
            pltpu.SemaphoreType.DMA((rows_all // rows,)),
            pltpu.SemaphoreType.DMA((num_states, parts)),
            pltpu.SemaphoreType.DMA,
            pltpu.SemaphoreType.DMA((2, parts)),
            pltpu.SemaphoreType.DMA((rows_all // rows, len(counts))),
        ],
        out_shape=[
            jax.ShapeDtypeStruct((count, num_states, rows_all * phys, chi), bf16)
            for count in counts
        ]
        + [TOKEN]
        + [share] * parts,
        compiler_params=pltpu.CompilerParams(vmem_limit_bytes=SWEEP_MIB * MIB),
        cost_estimate=pl.CostEstimate(
            flops=0,
            bytes_accessed=0,
            transcendentals=0,
        ),
        name="sweep",
    )(bonds, env, here, *[wave for turn in waves for wave in turn])
    pieces = len(counts)
    return out[:pieces], out[pieces], out[pieces + 1 :]


def applied_kernel(parts, pieces, begun, close, through_in, *refs):
    rights, refs = refs[: parts * pieces], refs[parts * pieces :]
    if begun:
        held, refs = refs[0], refs[1:]
    out, token_ref, turned, refs = refs[0], refs[1], refs[2], refs[3:]
    last = out.dtype == jnp.bfloat16
    count, num_states, rows, chi = through_in.shape
    if last:
        results, out_sems, refs = refs[0], refs[1], refs[2:]
    if close:
        through_ref = through_in
    else:
        through_ref, through_sems = refs

    def through_copies(k):
        return [
            pltpu.make_async_copy(through_in.at[v, k], through_ref.at[v, k], through_sems.at[v, k])
            for v in range(count)
        ]

    def out_copy(k, slot):
        return pltpu.make_async_copy(results.at[slot], out.at[k], out_sems.at[slot])

    if not close:
        for k in range(num_states):
            for copy in through_copies(k):
                copy.start()
    def turn(v):
        for piece in range(pieces):
            blocks = rights[piece * parts : (piece + 1) * parts]
            n = v - sum(rights[before * parts].shape[0] for before in range(piece))
            if 0 <= n < blocks[0].shape[0]:
                right = jnp.concatenate([block[n] for block in blocks], axis=0)
                turned[v * chi : (v + 1) * chi, :] = right.T

    def state(k, _):
        if not close:
            for copy in through_copies(k):
                copy.wait()
        if isinstance(k, int) and k == 0:
            total = None
            for v in range(0, count, 2):
                most = min(v + 2, count)
                for n in range(v, most):
                    turn(n)
                left = jnp.concatenate([through_ref[n, k] for n in range(v, most)], axis=1)
                term = product(left, turned[v * chi : most * chi, :], ((1,), (0,)))
                total = term if total is None else total + term
        else:
            left = jnp.concatenate([through_ref[v, k] for v in range(count)], axis=1)
            total = product(left, turned[...], ((1,), (0,)))
        if begun:
            total = total + held[k]
        if not last:
            out[k] = total
            return 0
        columns = total.shape[1]
        phys = results.shape[2]
        total = total.astype(jnp.bfloat16)
        if parts == 2:
            swap = lax.axis_index("bond") != 0
            total = own_first(swap, total[:, : columns // 2], total[:, columns // 2 :], 1)
        slot = k % 2

        if k >= 2:
            out_copy(k - 2, slot).wait()
        results[slot] = total.reshape(rows // phys, phys, columns)
        out_copy(k, slot).start()
        return 0

    state(0, 0)
    if last:
        for k in range(1, num_states):
            state(k, 0)
    else:
        lax.fori_loop(1, num_states, state, 0)
    if last:
        for k in range(max(num_states - 2, 0), num_states):
            out_copy(k, k % 2).wait()
    token_ref[...] = jnp.zeros_like(token_ref)


def applied_part(through, rights, held, phys, last):
    count, num_states, rows, chi = through.shape
    width = rights[0][0].shape[1]
    parts = len(rights[0])
    begun = held is not None
    close = count <= 4
    columns = width * parts
    scratch = [pltpu.VMEM((count * chi, columns), jnp.bfloat16)]
    if last:
        shape = (num_states, rows // phys, phys, columns)
        out_shape, out_spec = jax.ShapeDtypeStruct(shape, jnp.bfloat16), ANY
        scratch += [pltpu.VMEM((2,) + shape[1:], jnp.bfloat16), pltpu.SemaphoreType.DMA((2,))]
    else:
        out_shape, out_spec = pltpu.VMEM((num_states, rows, columns), jnp.float32), WHOLE
    if not close:
        scratch += [
            pltpu.VMEM(through.shape, jnp.bfloat16),
            pltpu.SemaphoreType.DMA((count, num_states)),
        ]
    operands = [near(through) if close else far(through)]
    operands += [near(block) for blocks in rights for block in blocks] + ([near(held)] if begun else [])
    return pl.pallas_call(
        functools.partial(applied_kernel, parts, len(rights), begun, close),
        in_specs=[WHOLE if close else ANY] + [WHOLE] * (len(operands) - 1),
        out_specs=[out_spec, WHOLE],
        out_shape=[out_shape, TOKEN],
        scratch_shapes=scratch,
        compiler_params=pltpu.CompilerParams(vmem_limit_bytes=(16 if close else 34) * MIB),
        cost_estimate=pl.CostEstimate(
            flops=0,
            bytes_accessed=0,
            transcendentals=0,
        ),
        name="applied_part",
    )(*operands)


def cuts(size):
    first = (size - 1) * 6 // 13
    return [[count] for count in (first, size - 1 - first, 1) if count > 0]


def on_device(left_env, right_env, states, mpo):
    num_states, rows, phys, chi = states.shape[1:]
    mw = mpo.shape[0]
    bonds = lax.axis_size("bond")
    paired = bonds == 2
    scaling = 1.0 / math.sqrt(num_states * chi)
    left = left_env[0].transpose(1, 0, 2)
    right = right_env[0].transpose(1, 0, 2)

    stages = cuts(mw)
    pieces, first = [], 0
    for stage in stages:
        pieces.append([])
        for count in stage:
            sent = right[first : first + count] if first else cut(right, first, count)
            piece = passed_along(sent, "seg", -1)
            pieces[-1].append(piece)
            first += count

    half = max(num_states // 2, 1)
    waves = []
    for start in range(0, num_states, half):
        wave = states[0, start : start + half].transpose(0, 2, 1, 3)
        if paired:
            waves.append([wave, swapped(wave, "bond")])
        else:
            waves.append([lax.all_gather(wave, "bond", axis=2, tiled=True)])
    bond_table = mpo.transpose(3, 1, 2, 0).reshape(mw * phys, phys * mw)
    counts = [sum(stage) for stage in stages]
    throughs, token, shares = sweep(bond_table, left, states, waves, counts, scaling)
    if paired:
        arrived = swapped(shares[1], "bond")
        new_env = shares[0].astype(jnp.float32) + arrived.astype(jnp.float32)
        new_env = new_env.astype(jnp.bfloat16)
    else:
        new_env = lax.psum_scatter(shares[0], "bond", scatter_dimension=1, tiled=True)

    held = None
    for index, (through, stage) in enumerate(zip(throughs, pieces)):
        rights = []
        for piece in stage:
            if paired:
                piece = after(piece, token)
                rights.append([piece, swapped(piece, "bond")])
            else:
                rights.append([lax.all_gather(piece, "bond", axis=1, tiled=True)])
        last = index == len(pieces) - 1
        held, token = applied_part(through, rights, held, phys, last)
    return (held[None], new_env.transpose(1, 0, 2)[None])


def solution(mesh):
    in_specs = (
        P("seg", "bond", None, None),
        P("seg", "bond", None, None),
        P("seg", None, "bond", None, None),
        P(),
    )
    out_specs = (P("seg", None, "bond", None, None), P("seg", "bond", None, None))
    return jax.shard_map(
        on_device, mesh=mesh, in_specs=in_specs, out_specs=out_specs, check_vma=False
    )
```

```python
import functools
import math

import jax
import jax.numpy as jnp
from jax import lax
from jax.experimental import pallas as pl
from jax.experimental.pallas import tpu as pltpu
from jax.sharding import PartitionSpec as P

GROUP = 8
MIB = 1 << 20
SWEEP_MIB = 56
ANY = pl.BlockSpec(memory_space=pl.ANY)
TOKEN = pltpu.VMEM((8, 128), jnp.float32)
WHOLE = pl.BlockSpec(memory_space=pltpu.VMEM)


def passed_along(array, axis, by):
    size = lax.axis_size(axis)
    pairs = [(i, i + by) for i in range(size) if 0 <= i + by < size]
    return lax.ppermute(array, axis, pairs)


def swapped(array, axis):
    return lax.ppermute(array, axis, [(0, 1), (1, 0)])


def product(left, right, contract):
    return lax.dot_general(left, right, (contract, ((), ())), preferred_element_type=jnp.float32)


def near(array):
    return pltpu.with_memory_space_constraint(array, pltpu.VMEM)


def far(array):
    return pltpu.with_memory_space_constraint(array, pltpu.HBM)


def after(array, token):
    return pl.pallas_call(
        lambda *refs: None,
        in_specs=[ANY, WHOLE],
        out_specs=ANY,
        out_shape=jax.ShapeDtypeStruct(array.shape, array.dtype),
        input_output_aliases={0: 0},
        compiler_params=pltpu.CompilerParams(vmem_limit_bytes=MIB),
        name="after",
    )(array, near(token))


def cut(array, at, count):
    def kernel(in_ref, out_ref, sems):
        copies = [
            pltpu.make_async_copy(in_ref.at[at + n], out_ref.at[n], sems.at[n])
            for n in range(count)
        ]
        for copy in copies:
            copy.start()
        for copy in copies:
            copy.wait()

    return pl.pallas_call(
        kernel,
        in_specs=[ANY],
        out_specs=WHOLE,
        out_shape=pltpu.VMEM((count,) + array.shape[1:], array.dtype),
        scratch_shapes=[pltpu.SemaphoreType.DMA((count,))],
        compiler_params=pltpu.CompilerParams(vmem_limit_bytes=8 * MIB),
        name="cut",
    )(far(array))


def block_diagonal(bonds, mw, phys):
    size = mw * phys
    full = size * GROUP
    row = lax.broadcasted_iota(jnp.int32, (full, size), 0)
    which = lax.broadcasted_iota(jnp.int32, (full, size), 1)
    pick_row = (row // (GROUP * phys) * phys + row % phys == which).astype(jnp.bfloat16)
    column = lax.broadcasted_iota(jnp.int32, (size, full), 1)
    which = lax.broadcasted_iota(jnp.int32, (size, full), 0)
    pick_column = (column // GROUP == which).astype(jnp.bfloat16)
    spread = product(pick_row, bonds, ((1,), (0,))).astype(jnp.bfloat16)
    spread = product(spread, pick_column, ((1,), (0,)))
    row = lax.broadcasted_iota(jnp.int32, (full, full), 0)
    column = lax.broadcasted_iota(jnp.int32, (full, full), 1)
    same = row % (GROUP * phys) // phys == column % GROUP
    return jnp.where(same, spread, 0.0).astype(jnp.bfloat16)


def own_first(swap, first, second, axis):
    return jnp.concatenate(
        [jnp.where(swap, second, first), jnp.where(swap, first, second)], axis=axis
    )


def sweep_kernel(parts, turns, pieces, scaling, bonds_ref, env_hbm, here_hbm, *refs):
    waves_hbm, refs = refs[: parts * turns], refs[parts * turns :]
    throughs_hbm, refs = refs[:pieces], refs[pieces:]
    token_ref, refs = refs[0], refs[1:]
    outs, refs = refs[:parts], refs[parts:]
    env_ref, here_ref, wave_ref, lhs, low, turned, stage, through_ref = refs[:8]
    env_sems, wave_sems, here_sem, out_sems, through_sems = refs[8:]
    mw, rows_all, chi_in = env_ref.shape
    num_states, phys, _, chi = wave_ref.shape
    width = chi_in // parts
    part = mw * GROUP
    groups = lhs.shape[0] // part
    rows = groups * GROUP
    blocks = rows_all // rows

    def env_copy(i):
        here = pl.ds(pl.multiple_of(i * rows, rows), rows)
        return pltpu.make_async_copy(env_hbm.at[:, here], env_ref.at[:, here], env_sems.at[i])

    def wave_starts(k):
        turn, inside = divmod(k, waves_hbm[0].shape[0])
        return [
            pltpu.make_async_copy(
                waves_hbm[turn * parts + index].at[inside],
                wave_ref.at[k, :, pl.ds(index * width, width)],
                wave_sems.at[k, index],
            )
            for index in range(parts)
        ]

    def wave_copies(k):
        return [
            pltpu.make_async_copy(
                waves_hbm[index].at[0],
                wave_ref.at[k, :, pl.ds(index * width, width)],
                wave_sems.at[k, index],
            )
            for index in range(parts)
        ]

    def through_copies(i):
        here = pl.ds(pl.multiple_of(i * rows * phys, rows * phys), rows * phys)
        found, first = [], 0
        for index, out in enumerate(throughs_hbm):
            count = out.shape[0]
            found.append(
                pltpu.make_async_copy(
                    through_ref.at[pl.ds(first, count), :, here],
                    out.at[:, :, here],
                    through_sems.at[i, index],
                )
            )
            first += count
        return found

    here_copy = pltpu.make_async_copy(here_hbm.at[0], here_ref, here_sem)
    for n in range(max(blocks, num_states)):
        if n < blocks:
            env_copy(n).start()
        if n < num_states:
            for copy in wave_starts(n):
                copy.start()
    here_copy.start()

    table = block_diagonal(bonds_ref[...], mw, phys)
    depth = table.shape[0]
    padded = low.shape[1]
    table = jnp.concatenate([table, jnp.zeros((depth, padded - depth), table.dtype)], axis=1)
    low[:, depth:, :] = jnp.zeros((groups, padded - depth, chi), low.dtype)
    swap = lax.axis_index("bond") != 0

    def block(i, _):
        env_copy(i).wait()
        env = env_ref[:, pl.ds(pl.multiple_of(i * rows, rows), rows), :].astype(jnp.float32)
        if parts == 2:
            env = own_first(swap, env[..., :width], env[..., width:], 2)
        env = env.reshape(mw, groups, GROUP, chi_in)
        for g in range(groups):
            lhs[g * part : (g + 1) * part, :] = env[:, g].reshape(part, chi_in).astype(jnp.bfloat16)

        def state(k, _):
            @pl.when(i == 0)
            def _():
                for copy in wave_copies(k):
                    copy.wait()

                @pl.when(k == 0)
                def _():
                    here_copy.wait()

            here = here_ref[k, pl.ds(pl.multiple_of(i * rows, rows), rows)]
            at = pl.multiple_of((k * blocks + i) * rows * phys, rows * phys)
            turned[:, pl.ds(at, rows * phys)] = here.reshape(rows * phys, chi).T
            for t in range(phys):
                inner = product(lhs[...], wave_ref[k, t], ((1,), (0,))).astype(jnp.bfloat16)
                low[:, t * part : (t + 1) * part, :] = inner.reshape(groups, part, chi)
            for g in range(groups):
                through = product(table, low[g], ((1,), (0,))).astype(jnp.bfloat16)
                size = GROUP * phys
                at = pl.multiple_of(i * rows * phys + g * size, size)
                through_ref[:, k, pl.ds(at, size), :] = through.reshape(mw, size, chi)
            return 0

        lax.fori_loop(0, num_states, state, 0)
        for copy in through_copies(i):
            copy.start()
        return 0

    lax.fori_loop(0, blocks, block, 0)

    depth = rows_all * phys

    def out_copies(v, slot):
        return [
            pltpu.make_async_copy(
                stage.at[slot, pl.ds(index * (chi // parts), chi // parts)],
                out.at[v],
                out_sems.at[slot, index],
            )
            for index, out in enumerate(outs)
        ]

    def bond(v, _):
        slot = v % 2
        right = through_ref[v].reshape(num_states * depth, chi)
        share = (product(turned[...], right, ((1,), (0,))) * scaling).astype(jnp.bfloat16)
        if parts == 2:
            share = own_first(swap, share[: chi // 2], share[chi // 2 :], 0)

        @pl.when(v >= 2)
        def _():
            for copy in out_copies(v - 2, slot):
                copy.wait()

        stage[slot] = share
        for copy in out_copies(v, slot):
            copy.start()
        return 0

    lax.fori_loop(0, mw, bond, 0)
    for v in range(max(mw - 2, 0), mw):
        for copy in out_copies(v, v % 2):
            copy.wait()
    for i in range(blocks):
        for copy in through_copies(i):
            copy.wait()
    token_ref[...] = jnp.zeros_like(token_ref)


def sweep(bonds, env, here, waves, counts, scaling):
    mw, rows_all, chi_in = env.shape
    phys, _, chi = waves[0][0].shape[1:]
    num_states = here.shape[1]
    rows = min(128, rows_all)
    parts = len(waves[0])
    padded = -(-mw * phys * GROUP // 128) * 128
    bf16 = jnp.bfloat16
    share = jax.ShapeDtypeStruct((mw, chi // parts, chi), bf16)
    out = pl.pallas_call(
        functools.partial(sweep_kernel, parts, len(waves), len(counts), scaling),
        in_specs=[WHOLE] + [ANY] * (2 + parts * len(waves)),
        out_specs=[ANY] * len(counts) + [WHOLE] + [ANY] * parts,
        scratch_shapes=[
            pltpu.VMEM(env.shape, bf16),
            pltpu.VMEM(here.shape[1:], bf16),
            pltpu.VMEM((num_states, phys, chi_in, chi), bf16),
            pltpu.VMEM((mw * rows, chi_in), bf16),
            pltpu.VMEM((rows // GROUP, padded, chi), bf16),
            pltpu.VMEM((chi, num_states * rows_all * phys), bf16),
            pltpu.VMEM((2, chi, chi), bf16),
            pltpu.VMEM((mw, num_states, rows_all * phys, chi), bf16),
            pltpu.SemaphoreType.DMA((rows_all // rows,)),
            pltpu.SemaphoreType.DMA((num_states, parts)),
            pltpu.SemaphoreType.DMA,
            pltpu.SemaphoreType.DMA((2, parts)),
            pltpu.SemaphoreType.DMA((rows_all // rows, len(counts))),
        ],
        out_shape=[
            jax.ShapeDtypeStruct((count, num_states, rows_all * phys, chi), bf16)
            for count in counts
        ]
        + [TOKEN]
        + [share] * parts,
        compiler_params=pltpu.CompilerParams(vmem_limit_bytes=SWEEP_MIB * MIB),
        cost_estimate=pl.CostEstimate(
            flops=0,
            bytes_accessed=0,
            transcendentals=0,
        ),
        name="sweep",
    )(bonds, env, here, *[wave for turn in waves for wave in turn])
    pieces = len(counts)
    return out[:pieces], out[pieces], out[pieces + 1 :]


def applied_kernel(parts, pieces, begun, close, through_in, *refs):
    rights, refs = refs[: parts * pieces], refs[parts * pieces :]
    if begun:
        held, refs = refs[0], refs[1:]
    out, token_ref, turned, refs = refs[0], refs[1], refs[2], refs[3:]
    last = out.dtype == jnp.bfloat16
    count, num_states, rows, chi = through_in.shape
    if last:
        results, out_sems, refs = refs[0], refs[1], refs[2:]
    if close:
        through_ref = through_in
    else:
        through_ref, through_sems = refs

    def through_copies(k):
        return [
            pltpu.make_async_copy(through_in.at[v, k], through_ref.at[v, k], through_sems.at[v, k])
            for v in range(count)
        ]

    def out_copy(k, slot):
        return pltpu.make_async_copy(results.at[slot], out.at[k], out_sems.at[slot])

    if not close:
        for k in range(num_states):
            for copy in through_copies(k):
                copy.start()
    def turn(v):
        for piece in range(pieces):
            blocks = rights[piece * parts : (piece + 1) * parts]
            n = v - sum(rights[before * parts].shape[0] for before in range(piece))
            if 0 <= n < blocks[0].shape[0]:
                right = jnp.concatenate([block[n] for block in blocks], axis=0)
                turned[v * chi : (v + 1) * chi, :] = right.T

    def state(k, _):
        if not close:
            for copy in through_copies(k):
                copy.wait()
        if isinstance(k, int) and k == 0:
            total = None
            for v in range(0, count, 2):
                most = min(v + 2, count)
                for n in range(v, most):
                    turn(n)
                left = jnp.concatenate([through_ref[n, k] for n in range(v, most)], axis=1)
                term = product(left, turned[v * chi : most * chi, :], ((1,), (0,)))
                total = term if total is None else total + term
        else:
            left = jnp.concatenate([through_ref[v, k] for v in range(count)], axis=1)
            total = product(left, turned[...], ((1,), (0,)))
        if begun:
            total = total + held[k]
        if not last:
            out[k] = total
            return 0
        columns = total.shape[1]
        phys = results.shape[2]
        total = total.astype(jnp.bfloat16)
        if parts == 2:
            swap = lax.axis_index("bond") != 0
            total = own_first(swap, total[:, : columns // 2], total[:, columns // 2 :], 1)
        slot = k % 2

        if k >= 2:
            out_copy(k - 2, slot).wait()
        results[slot] = total.reshape(rows // phys, phys, columns)
        out_copy(k, slot).start()
        return 0

    state(0, 0)
    if last:
        for k in range(1, num_states):
            state(k, 0)
    else:
        lax.fori_loop(1, num_states, state, 0)
    if last:
        for k in range(max(num_states - 2, 0), num_states):
            out_copy(k, k % 2).wait()
    token_ref[...] = jnp.zeros_like(token_ref)


def applied_part(through, rights, held, phys, last):
    count, num_states, rows, chi = through.shape
    width = rights[0][0].shape[1]
    parts = len(rights[0])
    begun = held is not None
    close = count <= 4
    columns = width * parts
    scratch = [pltpu.VMEM((count * chi, columns), jnp.bfloat16)]
    if last:
        shape = (num_states, rows // phys, phys, columns)
        out_shape, out_spec = jax.ShapeDtypeStruct(shape, jnp.bfloat16), ANY
        scratch += [pltpu.VMEM((2,) + shape[1:], jnp.bfloat16), pltpu.SemaphoreType.DMA((2,))]
    else:
        out_shape, out_spec = pltpu.VMEM((num_states, rows, columns), jnp.float32), WHOLE
    if not close:
        scratch += [
            pltpu.VMEM(through.shape, jnp.bfloat16),
            pltpu.SemaphoreType.DMA((count, num_states)),
        ]
    operands = [near(through) if close else far(through)]
    operands += [near(block) for blocks in rights for block in blocks] + ([near(held)] if begun else [])
    return pl.pallas_call(
        functools.partial(applied_kernel, parts, len(rights), begun, close),
        in_specs=[WHOLE if close else ANY] + [WHOLE] * (len(operands) - 1),
        out_specs=[out_spec, WHOLE],
        out_shape=[out_shape, TOKEN],
        scratch_shapes=scratch,
        compiler_params=pltpu.CompilerParams(vmem_limit_bytes=(16 if close else 34) * MIB),
        cost_estimate=pl.CostEstimate(
            flops=0,
            bytes_accessed=0,
            transcendentals=0,
        ),
        name="applied_part",
    )(*operands)


def cuts(size):
    first = (size - 1) * 6 // 13
    return [[count] for count in (first, size - 1 - first, 1) if count > 0]


def on_device(left_env, right_env, states, mpo):
    num_states, rows, phys, chi = states.shape[1:]
    mw = mpo.shape[0]
    bonds = lax.axis_size("bond")
    paired = bonds == 2
    scaling = 1.0 / math.sqrt(num_states * chi)
    left = left_env[0].transpose(1, 0, 2)
    right = right_env[0].transpose(1, 0, 2)

    stages = cuts(mw)
    pieces, first = [], 0
    for stage in stages:
        pieces.append([])
        for count in stage:
            sent = right[first : first + count] if first else cut(right, first, count)
            piece = passed_along(sent, "seg", -1)
            pieces[-1].append(piece)
            first += count

    half = max(num_states // 2, 1)
    waves = []
    for start in range(0, num_states, half):
        wave = states[0, start : start + half].transpose(0, 2, 1, 3)
        if paired:
            waves.append([wave, swapped(wave, "bond")])
        else:
            waves.append([lax.all_gather(wave, "bond", axis=2, tiled=True)])
    bond_table = mpo.transpose(3, 1, 2, 0).reshape(mw * phys, phys * mw)
    counts = [sum(stage) for stage in stages]
    throughs, token, shares = sweep(bond_table, left, states, waves, counts, scaling)
    if paired:
        arrived = swapped(shares[1], "bond")
        new_env = shares[0].astype(jnp.float32) + arrived.astype(jnp.float32)
        new_env = new_env.astype(jnp.bfloat16)
    else:
        new_env = lax.psum_scatter(shares[0], "bond", scatter_dimension=1, tiled=True)

    held = None
    for index, (through, stage) in enumerate(zip(throughs, pieces)):
        rights = []
        for piece in stage:
            if paired:
                piece = after(piece, token)
                rights.append([piece, swapped(piece, "bond")])
            else:
                rights.append([lax.all_gather(piece, "bond", axis=1, tiled=True)])
        last = index == len(pieces) - 1
        held, token = applied_part(through, rights, held, phys, last)
    return (held[None], new_env.transpose(1, 0, 2)[None])


def solution(mesh):
    in_specs = (
        P("seg", "bond", None, None),
        P("seg", "bond", None, None),
        P("seg", None, "bond", None, None),
        P(),
    )
    out_specs = (P("seg", None, "bond", None, None), P("seg", "bond", None, None))
    return jax.shard_map(
        on_device, mesh=mesh, in_specs=in_specs, out_specs=out_specs, check_vma=False
    )
```

```python
import functools
import math

import jax
import jax.numpy as jnp
from jax import lax
from jax.experimental import pallas as pl
from jax.experimental.pallas import tpu as pltpu
from jax.sharding import PartitionSpec as P

GROUP = 8
MIB = 1 << 20
SWEEP_MIB = 54
ANY = pl.BlockSpec(memory_space=pl.ANY)
TOKEN = pltpu.VMEM((8, 128), jnp.float32)
WHOLE = pl.BlockSpec(memory_space=pltpu.VMEM)


def passed_along(array, axis, by):
    size = lax.axis_size(axis)
    pairs = [(i, i + by) for i in range(size) if 0 <= i + by < size]
    return lax.ppermute(array, axis, pairs)


def swapped(array, axis):
    return lax.ppermute(array, axis, [(0, 1), (1, 0)])


def product(left, right, contract):
    return lax.dot_general(left, right, (contract, ((), ())), preferred_element_type=jnp.float32)


def near(array):
    return pltpu.with_memory_space_constraint(array, pltpu.VMEM)


def far(array):
    return pltpu.with_memory_space_constraint(array, pltpu.HBM)


def after(array, token):
    return pl.pallas_call(
        lambda *refs: None,
        in_specs=[ANY, WHOLE],
        out_specs=ANY,
        out_shape=jax.ShapeDtypeStruct(array.shape, array.dtype),
        input_output_aliases={0: 0},
        compiler_params=pltpu.CompilerParams(vmem_limit_bytes=MIB),
        name="after",
    )(array, near(token))


def cut(array, at, count):
    def kernel(in_ref, out_ref, sems):
        copies = [
            pltpu.make_async_copy(in_ref.at[at + n], out_ref.at[n], sems.at[n])
            for n in range(count)
        ]
        for copy in copies:
            copy.start()
        for copy in copies:
            copy.wait()

    return pl.pallas_call(
        kernel,
        in_specs=[ANY],
        out_specs=WHOLE,
        out_shape=pltpu.VMEM((count,) + array.shape[1:], array.dtype),
        scratch_shapes=[pltpu.SemaphoreType.DMA((count,))],
        compiler_params=pltpu.CompilerParams(vmem_limit_bytes=8 * MIB),
        name="cut",
    )(far(array))


def block_diagonal(bonds, mw, phys):
    size = mw * phys
    full = size * GROUP
    row = lax.broadcasted_iota(jnp.int32, (full, size), 0)
    which = lax.broadcasted_iota(jnp.int32, (full, size), 1)
    pick_row = (row // (GROUP * phys) * phys + row % phys == which).astype(jnp.bfloat16)
    column = lax.broadcasted_iota(jnp.int32, (size, full), 1)
    which = lax.broadcasted_iota(jnp.int32, (size, full), 0)
    pick_column = (column // GROUP == which).astype(jnp.bfloat16)
    spread = product(pick_row, bonds, ((1,), (0,))).astype(jnp.bfloat16)
    spread = product(spread, pick_column, ((1,), (0,)))
    row = lax.broadcasted_iota(jnp.int32, (full, full), 0)
    column = lax.broadcasted_iota(jnp.int32, (full, full), 1)
    same = row % (GROUP * phys) // phys == column % GROUP
    return jnp.where(same, spread, 0.0).astype(jnp.bfloat16)


def own_first(swap, first, second, axis):
    return jnp.concatenate(
        [jnp.where(swap, second, first), jnp.where(swap, first, second)], axis=axis
    )


def sweep_kernel(parts, turns, pieces, scaling, bonds_ref, env_hbm, here_hbm, *refs):
    waves_hbm, refs = refs[: parts * turns], refs[parts * turns :]
    throughs_hbm, refs = refs[:pieces], refs[pieces:]
    token_ref, refs = refs[0], refs[1:]
    outs, refs = refs[:parts], refs[parts:]
    env_ref, here_ref, wave_ref, lhs, low, turned, stage, through_ref = refs[:8]
    env_sems, wave_sems, here_sem, out_sems, through_sems = refs[8:]
    mw, rows_all, chi_in = env_ref.shape
    num_states, phys, _, chi = wave_ref.shape
    width = chi_in // parts
    part = mw * GROUP
    groups = lhs.shape[0] // part
    rows = groups * GROUP
    blocks = rows_all // rows

    def env_copy(i):
        here = pl.ds(pl.multiple_of(i * rows, rows), rows)
        return pltpu.make_async_copy(env_hbm.at[:, here], env_ref.at[:, here], env_sems.at[i])

    def wave_starts(k):
        turn, inside = divmod(k, waves_hbm[0].shape[0])
        return [
            pltpu.make_async_copy(
                waves_hbm[turn * parts + index].at[inside],
                wave_ref.at[k, :, pl.ds(index * width, width)],
                wave_sems.at[k, index],
            )
            for index in range(parts)
        ]

    def wave_copies(k):
        return [
            pltpu.make_async_copy(
                waves_hbm[index].at[0],
                wave_ref.at[k, :, pl.ds(index * width, width)],
                wave_sems.at[k, index],
            )
            for index in range(parts)
        ]

    def through_copies(i):
        here = pl.ds(pl.multiple_of(i * rows * phys, rows * phys), rows * phys)
        found, first = [], 0
        for index, out in enumerate(throughs_hbm):
            count = out.shape[0]
            found.append(
                pltpu.make_async_copy(
                    through_ref.at[pl.ds(first, count), :, here],
                    out.at[:, :, here],
                    through_sems.at[i, index],
                )
            )
            first += count
        return found

    here_copy = pltpu.make_async_copy(here_hbm.at[0], here_ref, here_sem)
    for n in range(max(blocks, num_states)):
        if n < blocks:
            env_copy(n).start()
        if n < num_states:
            for copy in wave_starts(n):
                copy.start()
    here_copy.start()

    table = block_diagonal(bonds_ref[...], mw, phys)
    depth = table.shape[0]
    padded = low.shape[1]
    table = jnp.concatenate([table, jnp.zeros((depth, padded - depth), table.dtype)], axis=1)
    low[:, depth:, :] = jnp.zeros((groups, padded - depth, chi), low.dtype)
    swap = lax.axis_index("bond") != 0

    def block(i, _):
        env_copy(i).wait()
        env = env_ref[:, pl.ds(pl.multiple_of(i * rows, rows), rows), :].astype(jnp.float32)
        if parts == 2:
            env = own_first(swap, env[..., :width], env[..., width:], 2)
        env = env.reshape(mw, groups, GROUP, chi_in)
        for g in range(groups):
            lhs[g * part : (g + 1) * part, :] = env[:, g].reshape(part, chi_in).astype(jnp.bfloat16)

        def state(k, _):
            @pl.when(i == 0)
            def _():
                for copy in wave_copies(k):
                    copy.wait()

                @pl.when(k == 0)
                def _():
                    here_copy.wait()

            here = here_ref[k, pl.ds(pl.multiple_of(i * rows, rows), rows)]
            at = pl.multiple_of((k * blocks + i) * rows * phys, rows * phys)
            turned[:, pl.ds(at, rows * phys)] = here.reshape(rows * phys, chi).T
            for t in range(phys):
                inner = product(lhs[...], wave_ref[k, t], ((1,), (0,))).astype(jnp.bfloat16)
                low[:, t * part : (t + 1) * part, :] = inner.reshape(groups, part, chi)
            for g in range(groups):
                through = product(table, low[g], ((1,), (0,))).astype(jnp.bfloat16)
                size = GROUP * phys
                at = pl.multiple_of(i * rows * phys + g * size, size)
                through_ref[:, k, pl.ds(at, size), :] = through.reshape(mw, size, chi)
            return 0

        lax.fori_loop(0, num_states, state, 0)
        for copy in through_copies(i):
            copy.start()
        return 0

    lax.fori_loop(0, blocks, block, 0)

    depth = rows_all * phys

    def out_copies(v, slot):
        return [
            pltpu.make_async_copy(
                stage.at[slot, pl.ds(index * (chi // parts), chi // parts)],
                out.at[v],
                out_sems.at[slot, index],
            )
            for index, out in enumerate(outs)
        ]

    def bond(v, _):
        slot = v % 2
        right = through_ref[v].reshape(num_states * depth, chi)
        share = (product(turned[...], right, ((1,), (0,))) * scaling).astype(jnp.bfloat16)
        if parts == 2:
            share = own_first(swap, share[: chi // 2], share[chi // 2 :], 0)

        @pl.when(v >= 2)
        def _():
            for copy in out_copies(v - 2, slot):
                copy.wait()

        stage[slot] = share
        for copy in out_copies(v, slot):
            copy.start()
        return 0

    lax.fori_loop(0, mw, bond, 0)
    for v in range(max(mw - 2, 0), mw):
        for copy in out_copies(v, v % 2):
            copy.wait()
    for i in range(blocks):
        for copy in through_copies(i):
            copy.wait()
    token_ref[...] = jnp.zeros_like(token_ref)


def sweep(bonds, env, here, waves, counts, scaling):
    mw, rows_all, chi_in = env.shape
    phys, _, chi = waves[0][0].shape[1:]
    num_states = here.shape[1]
    rows = min(64, rows_all)
    parts = len(waves[0])
    padded = -(-mw * phys * GROUP // 128) * 128
    bf16 = jnp.bfloat16
    share = jax.ShapeDtypeStruct((mw, chi // parts, chi), bf16)
    out = pl.pallas_call(
        functools.partial(sweep_kernel, parts, len(waves), len(counts), scaling),
        in_specs=[WHOLE] + [ANY] * (2 + parts * len(waves)),
        out_specs=[ANY] * len(counts) + [WHOLE] + [ANY] * parts,
        scratch_shapes=[
            pltpu.VMEM(env.shape, bf16),
            pltpu.VMEM(here.shape[1:], bf16),
            pltpu.VMEM((num_states, phys, chi_in, chi), bf16),
            pltpu.VMEM((mw * rows, chi_in), bf16),
            pltpu.VMEM((rows // GROUP, padded, chi), bf16),
            pltpu.VMEM((chi, num_states * rows_all * phys), bf16),
            pltpu.VMEM((2, chi, chi), bf16),
            pltpu.VMEM((mw, num_states, rows_all * phys, chi), bf16),
            pltpu.SemaphoreType.DMA((rows_all // rows,)),
            pltpu.SemaphoreType.DMA((num_states, parts)),
            pltpu.SemaphoreType.DMA,
            pltpu.SemaphoreType.DMA((2, parts)),
            pltpu.SemaphoreType.DMA((rows_all // rows, len(counts))),
        ],
        out_shape=[
            jax.ShapeDtypeStruct((count, num_states, rows_all * phys, chi), bf16)
            for count in counts
        ]
        + [TOKEN]
        + [share] * parts,
        compiler_params=pltpu.CompilerParams(vmem_limit_bytes=SWEEP_MIB * MIB),
        cost_estimate=pl.CostEstimate(
            flops=0,
            bytes_accessed=0,
            transcendentals=0,
        ),
        name="sweep",
    )(bonds, env, here, *[wave for turn in waves for wave in turn])
    pieces = len(counts)
    return out[:pieces], out[pieces], out[pieces + 1 :]


def applied_kernel(parts, pieces, begun, close, through_in, *refs):
    rights, refs = refs[: parts * pieces], refs[parts * pieces :]
    if begun:
        held, refs = refs[0], refs[1:]
    out, token_ref, turned, refs = refs[0], refs[1], refs[2], refs[3:]
    last = out.dtype == jnp.bfloat16
    count, num_states, rows, chi = through_in.shape
    if last:
        results, out_sems, refs = refs[0], refs[1], refs[2:]
    if close:
        through_ref = through_in
    else:
        through_ref, through_sems = refs

    def through_copies(k):
        return [
            pltpu.make_async_copy(through_in.at[v, k], through_ref.at[v, k], through_sems.at[v, k])
            for v in range(count)
        ]

    def out_copy(k, slot):
        return pltpu.make_async_copy(results.at[slot], out.at[k], out_sems.at[slot])

    if not close:
        for k in range(num_states):
            for copy in through_copies(k):
                copy.start()
    def turn(v):
        for piece in range(pieces):
            blocks = rights[piece * parts : (piece + 1) * parts]
            n = v - sum(rights[before * parts].shape[0] for before in range(piece))
            if 0 <= n < blocks[0].shape[0]:
                right = jnp.concatenate([block[n] for block in blocks], axis=0)
                turned[v * chi : (v + 1) * chi, :] = right.T

    def state(k, _):
        if not close:
            for copy in through_copies(k):
                copy.wait()
        if isinstance(k, int) and k == 0:
            total = None
            for v in range(0, count, 2):
                most = min(v + 2, count)
                for n in range(v, most):
                    turn(n)
                left = jnp.concatenate([through_ref[n, k] for n in range(v, most)], axis=1)
                term = product(left, turned[v * chi : most * chi, :], ((1,), (0,)))
                total = term if total is None else total + term
        else:
            left = jnp.concatenate([through_ref[v, k] for v in range(count)], axis=1)
            total = product(left, turned[...], ((1,), (0,)))
        if begun:
            total = total + held[k]
        if not last:
            out[k] = total
            return 0
        columns = total.shape[1]
        phys = results.shape[2]
        total = total.astype(jnp.bfloat16)
        if parts == 2:
            swap = lax.axis_index("bond") != 0
            total = own_first(swap, total[:, : columns // 2], total[:, columns // 2 :], 1)
        slot = k % 2

        if k >= 2:
            out_copy(k - 2, slot).wait()
        results[slot] = total.reshape(rows // phys, phys, columns)
        out_copy(k, slot).start()
        return 0

    state(0, 0)
    for k in range(1, num_states):
        state(k, 0)
    if last:
        for k in range(max(num_states - 2, 0), num_states):
            out_copy(k, k % 2).wait()
    token_ref[...] = jnp.zeros_like(token_ref)


def applied_part(through, rights, held, phys, last):
    count, num_states, rows, chi = through.shape
    width = rights[0][0].shape[1]
    parts = len(rights[0])
    begun = held is not None
    close = count <= 4
    columns = width * parts
    scratch = [pltpu.VMEM((count * chi, columns), jnp.bfloat16)]
    if last:
        shape = (num_states, rows // phys, phys, columns)
        out_shape, out_spec = jax.ShapeDtypeStruct(shape, jnp.bfloat16), ANY
        scratch += [pltpu.VMEM((2,) + shape[1:], jnp.bfloat16), pltpu.SemaphoreType.DMA((2,))]
    else:
        out_shape, out_spec = pltpu.VMEM((num_states, rows, columns), jnp.float32), WHOLE
    if not close:
        scratch += [
            pltpu.VMEM(through.shape, jnp.bfloat16),
            pltpu.SemaphoreType.DMA((count, num_states)),
        ]
    operands = [near(through) if close else far(through)]
    operands += [near(block) for blocks in rights for block in blocks] + ([near(held)] if begun else [])
    return pl.pallas_call(
        functools.partial(applied_kernel, parts, len(rights), begun, close),
        in_specs=[WHOLE if close else ANY] + [WHOLE] * (len(operands) - 1),
        out_specs=[out_spec, WHOLE],
        out_shape=[out_shape, TOKEN],
        scratch_shapes=scratch,
        compiler_params=pltpu.CompilerParams(vmem_limit_bytes=(16 if close else 34) * MIB),
        cost_estimate=pl.CostEstimate(
            flops=0,
            bytes_accessed=0,
            transcendentals=0,
        ),
        name="applied_part",
    )(*operands)


def cuts(size):
    first = (size - 1) * 6 // 13
    return [[count] for count in (first, size - 1 - first, 1) if count > 0]


def on_device(left_env, right_env, states, mpo):
    num_states, rows, phys, chi = states.shape[1:]
    mw = mpo.shape[0]
    bonds = lax.axis_size("bond")
    paired = bonds == 2
    scaling = 1.0 / math.sqrt(num_states * chi)
    left = left_env[0].transpose(1, 0, 2)
    right = right_env[0].transpose(1, 0, 2)

    stages = cuts(mw)
    pieces, first = [], 0
    for stage in stages:
        pieces.append([])
        for count in stage:
            sent = right[first : first + count] if first else cut(right, first, count)
            piece = passed_along(sent, "seg", -1)
            pieces[-1].append(piece)
            first += count

    half = max(num_states // 2, 1)
    waves = []
    for start in range(0, num_states, half):
        wave = states[0, start : start + half].transpose(0, 2, 1, 3)
        if paired:
            waves.append([wave, swapped(wave, "bond")])
        else:
            waves.append([lax.all_gather(wave, "bond", axis=2, tiled=True)])
    bond_table = mpo.transpose(3, 1, 2, 0).reshape(mw * phys, phys * mw)
    counts = [sum(stage) for stage in stages]
    throughs, token, shares = sweep(bond_table, left, states, waves, counts, scaling)
    if paired:
        arrived = swapped(shares[1], "bond")
        new_env = shares[0].astype(jnp.float32) + arrived.astype(jnp.float32)
        new_env = new_env.astype(jnp.bfloat16)
    else:
        new_env = lax.psum_scatter(shares[0], "bond", scatter_dimension=1, tiled=True)

    held = None
    for index, (through, stage) in enumerate(zip(throughs, pieces)):
        rights = []
        for piece in stage:
            if paired:
                piece = after(piece, token)
                rights.append([piece, swapped(piece, "bond")])
            else:
                rights.append([lax.all_gather(piece, "bond", axis=1, tiled=True)])
        last = index == len(pieces) - 1
        held, token = applied_part(through, rights, held, phys, last)
    return (held[None], new_env.transpose(1, 0, 2)[None])


def solution(mesh):
    in_specs = (
        P("seg", "bond", None, None),
        P("seg", "bond", None, None),
        P("seg", None, "bond", None, None),
        P(),
    )
    out_specs = (P("seg", None, "bond", None, None), P("seg", "bond", None, None))
    return jax.shard_map(
        on_device, mesh=mesh, in_specs=in_specs, out_specs=out_specs, check_vma=False
    )
```
